32 devices in a mesh: gz: 8 (over z, y), phi: 4 (over x, core).
Axes of the slice: x: 2, y: 2, z: 4, core: 2. Of those that a mesh axis runs over, the one named last changes fastest.
Arguments:
- field: float32 [16, 4, 2048, 1024], P(None, None, 'gz', 'phi'), may hold values from -6 to 6
- field_tangent: float32 [16, 4, 2048, 1024], P(None, None, 'gz', 'phi'), may hold values from -6 to 6
- spectral_weight: float32 [2, 16, 16, 64, 64], P(None, None, None, 'gz', 'phi'), may hold values from -1 to 1
- local_weight: float32 [16, 16], replicated, may hold values from -1.5 to 1.5
- bias_term: float32 [16], replicated, may hold values from -3 to 3
- z_modes: int32 [64], replicated, may hold values from 0 to 1023, as said below
- phi_modes: int32 [64], replicated, may hold values from 0 to 1023, as said below
Outputs:
- output: float32 [16, 4, 2048, 1024], P(None, None, 'gz', 'phi')
- output_tangent: float32 [16, 4, 2048, 1024], P(None, None, 'gz', 'phi')
The draws below stay inside these ranges and needn't reach their ends.
Inputs may be any that keep to these rules, and one draw needn't show every extreme that they name: `z_modes`: entries may repeat; 0 and 1023 both occur. `phi_modes`: entries may repeat; 0 and 1023 both occur.
All inputs are finite; a program needn't handle non-finite values.
Results may differ from the reference program's by a relative error of at most 0.000078.
Values sent between devices are 32-bit elements; how exact they have to be, the bound alone decides.
No kernel may reach another device: no remote copies, remote signals or barrier semaphores. Data moves between devices by JAX's collectives and lax.ppermute only.
A program may use at most 256 MiB of HBM per device.

```python
import functools
import math
import jax
import jax.numpy as jnp
from jax import lax

C = 16
CYCLE = 4
Z = 2048
PHI = 1024
KZ = 64
KP = 64


def place_ends(key, count, upper):
    values = jax.random.randint(key, (count,), 0, upper, dtype=jnp.int32)
    slots = jax.random.permutation(jax.random.fold_in(key, 7), count)
    return values.at[slots[0]].set(0).at[slots[1]].set(upper - 1)


def draw_z_modes(key, part):
    return place_ends(jax.random.fold_in(key, 11), KZ, Z // 2)


def draw_phi_modes(key, part):
    return place_ends(jax.random.fold_in(key, 13), KP, PHI)


def level_of(stream_key, dims, shards, low, largest):
    level = 1.0
    for axis_at, shards_of in shards:
        heights = jax.random.uniform(jax.random.fold_in(jax.random.fold_in(stream_key, 6), axis_at), (shards_of,), jnp.float32, low / len(shards), largest / len(shards))
        level = level * jnp.repeat(jnp.exp(heights), dims[axis_at] // shards_of).reshape((-1,) + (1,) * (len(dims) - 1 - axis_at))
    return level


def gaussian(stream_key, extent, spread, limit, pieces=(), kind=jnp.bfloat16):
    values = spread * jax.random.normal(stream_key, extent, jnp.float32)
    if pieces:
        values = values * level_of(stream_key, extent, pieces, -0.22, 0.18)
    return jnp.clip(values, -limit, limit).astype(kind)


def setup_inputs(seed: int = 0) -> dict:
    keys = jax.random.split(jax.random.key(seed), 8)
    return {
        "field": gaussian(keys[0], (C, CYCLE, Z, PHI), 1.0, 6.0, ((2, 8), (3, 4)), jnp.float32),
        "field_tangent": gaussian(keys[1], (C, CYCLE, Z, PHI), 1.0, 6.0, ((2, 8), (3, 4)), jnp.float32),
        "spectral_weight": gaussian(keys[2], (2, C, C, KZ, KP), (2 * C) ** -0.5, 1.0, ((3, 8), (4, 4)), jnp.float32),
        "local_weight": gaussian(keys[3], (C, C), C ** -0.5, 1.5, (), jnp.float32),
        "bias_term": gaussian(keys[4], (C,), 0.5, 3.0, (), jnp.float32),
        "z_modes": draw_z_modes(jax.random.fold_in(keys[7], 71), 0),
        "phi_modes": draw_phi_modes(jax.random.fold_in(keys[7], 71), 0),
    }


precise = lax.Precision.HIGHEST

def angle_table(positions, modes, length):
    product = positions[:, None] * modes[None, :] % length
    angle = product.astype(jnp.float32) * (2.0 * math.pi / length)
    return (jnp.cos(angle), jnp.sin(angle))

def cycle_layer(stacked, spectral_weight, local_weight, bias_term, z_modes, phi_modes):
    z_cosine, z_sine = angle_table(jnp.arange(Z, dtype=jnp.int32), z_modes, Z)
    p_cosine, p_sine = angle_table(jnp.arange(PHI, dtype=jnp.int32), phi_modes, PHI)
    zreal = jnp.einsum('pczf,zk->pckf', stacked, z_cosine, precision=precise)
    zimag = -jnp.einsum('pczf,zk->pckf', stacked, z_sine, precision=precise)
    scaling = 1.0 / math.sqrt(Z * PHI)
    freal = (jnp.einsum('pckf,fq->pckq', zreal, p_cosine, precision=precise) + jnp.einsum('pckf,fq->pckq', zimag, p_sine, precision=precise)) * scaling
    fimag = (jnp.einsum('pckf,fq->pckq', zimag, p_cosine, precision=precise) - jnp.einsum('pckf,fq->pckq', zreal, p_sine, precision=precise)) * scaling
    wreal = spectral_weight[0]
    wimag = spectral_weight[1]
    greal = jnp.einsum('pckq,cokq->pokq', freal, wreal, precision=precise) - jnp.einsum('pckq,cokq->pokq', fimag, wimag, precision=precise)
    gimag = jnp.einsum('pckq,cokq->pokq', fimag, wreal, precision=precise) + jnp.einsum('pckq,cokq->pokq', freal, wimag, precision=precise)
    hreal = jnp.einsum('pokq,fq->pokf', greal, p_cosine, precision=precise) - jnp.einsum('pokq,fq->pokf', gimag, p_sine, precision=precise)
    himag = jnp.einsum('pokq,fq->pokf', greal, p_sine, precision=precise) + jnp.einsum('pokq,fq->pokf', gimag, p_cosine, precision=precise)
    spectral = (jnp.einsum('pokf,zk->pozf', hreal, z_cosine, precision=precise) - jnp.einsum('pokf,zk->pozf', himag, z_sine, precision=precise)) * (2.0 / math.sqrt(KZ * KP))
    mixing = jnp.einsum('pczf,co->pozf', stacked, local_weight, precision=precise)
    preact = spectral[0] + mixing[0] + bias_term[:, None, None]
    tangent = spectral[1] + mixing[1]
    return jax.jvp(functools.partial(jax.nn.gelu, approximate=True), (preact,), (tangent,))

def reference(field, field_tangent, spectral_weight, local_weight, bias_term, z_modes, phi_modes):

    def one_cycle(index):
        stacked = jnp.stack([lax.dynamic_index_in_dim(field, index, 1, keepdims=False), lax.dynamic_index_in_dim(field_tangent, index, 1, keepdims=False)])
        return cycle_layer(stacked, spectral_weight, local_weight, bias_term, z_modes, phi_modes)
    output, output_tangent = lax.map(one_cycle, jnp.arange(CYCLE, dtype=jnp.int32))
    return (jnp.swapaxes(output, 0, 1), jnp.swapaxes(output_tangent, 0, 1))
```

```python
import functools
import itertools
import math

import jax
import jax.numpy as jnp
from jax import lax
from jax.experimental import pallas as pl
from jax.experimental.pallas import tpu as pltpu
from jax.sharding import PartitionSpec as P

f32 = jnp.float32
bf16 = jnp.bfloat16
VMEM_LIMIT = 56 * 1024 * 1024


def split(x):
    high = lax.reduce_precision(x, 8, 7)
    return high.astype(bf16), (x - high).astype(bf16)


def halves(x):
    high = x.astype(bf16)
    return high, (x - high.astype(f32)).astype(bf16)


def dot(a, b):
    return lax.dot_general(a, b, (((1,), (0,)), ((), ())), preferred_element_type=f32)


def angles(positions, modes, length):
    product = positions[:, None] * modes[None, :] % length
    angle = product.astype(f32) * (2.0 * math.pi / length)
    return jnp.cos(angle), jnp.sin(angle)


def exchange(items, width):
    items = list(items)
    count = len(items)
    lanes = items[0].shape[-1]
    lane = lax.broadcasted_iota(jnp.int32, items[0].shape, items[0].ndim - 1)
    step = 1
    while step < count:
        shift = width * step
        low = (lane // shift) % 2 == 0
        for i in range(count):
            if i & step:
                continue
            a, b = items[i], items[i | step]
            items[i] = jnp.where(low, a, pltpu.roll(b, shift, 1))
            items[i | step] = jnp.where(low, pltpu.roll(a, lanes - shift, 1), b)
        step *= 2
    return items


def forward_kernel(x_ref, t_ref, phi_ref, z_ref, keep_ref, send_ref, *, n_phi, width):
    cycles, z_local, _ = x_ref.shape[1:]
    modes2 = z_ref.shape[0] // 2
    modes = modes2 // 2
    lanes = phi_ref.shape[1] // 2
    lane = lax.broadcasted_iota(jnp.int32, (modes, lanes), 1)
    sign = jnp.where(lane < lanes // 2, 1.0, -1.0).astype(f32)
    batch = [(ref, r) for ref in (x_ref, t_ref) for r in range(cycles)]
    for group in range(len(batch) // n_phi):
        items = []
        for ref, r in batch[group * n_phi : (group + 1) * n_phi]:
            high, low = halves(ref[0, r])
            y = dot(jnp.concatenate([high, low], axis=1), phi_ref[...])
            y = y[:, :lanes] + y[:, lanes:]
            y_high, y_low = halves(y)
            m = dot(z_ref[...], jnp.concatenate([y_high, y_low], axis=1))
            m = m[:modes2, :lanes] + (m[:modes2, lanes:] + m[modes2:, :lanes])
            items.append(m[:modes] + sign * pltpu.roll(m[modes:], lanes // 2, 1))
        items = exchange(items, width)
        shape = keep_ref.shape[1:-4] + keep_ref.shape[-2:]
        for slot, item in enumerate(items):
            out = keep_ref if slot % 2 == 0 else send_ref
            out[slot // 2, ..., 0, group, :, :] = item.reshape(shape)


def forward(field, tangent, phi_table, z_table, n_phi, n_gz, width):
    channels, cycles, z_local, phi_local = field.shape
    groups = 2 * cycles // n_phi
    modes = z_table.shape[0] // 4
    lanes = phi_table.shape[1] // 2
    out = jax.ShapeDtypeStruct((n_phi // 2, n_gz, channels, groups, modes // n_gz, lanes), f32)
    block = pl.BlockSpec((1, cycles, z_local, phi_local), lambda c: (c, 0, 0, 0))
    out_block = pl.BlockSpec(
        (n_phi // 2, n_gz, 1, groups, modes // n_gz, lanes), lambda c: (0, 0, c, 0, 0, 0)
    )
    return pl.pallas_call(
        functools.partial(forward_kernel, n_phi=n_phi, width=width),
        grid=(channels,),
        in_specs=[
            block,
            block,
            pl.BlockSpec(phi_table.shape, lambda c: (0, 0)),
            pl.BlockSpec(z_table.shape, lambda c: (0, 0)),
        ],
        out_specs=[out_block, out_block],
        out_shape=[out, out],
        compiler_params=pltpu.CompilerParams(vmem_limit_bytes=VMEM_LIMIT),
        cost_estimate=pl.CostEstimate(
            flops=12 * field.size * phi_table.shape[1],
            bytes_accessed=8 * field.size,
            transcendentals=0,
        ),
        name="forward_transform",
    )(field, tangent, phi_table, z_table)


def local_kernel(x_ref, t_ref, w_ref, xo_ref, to_ref):
    channels, _, rows, columns = x_ref.shape
    for ref, out in ((x_ref, xo_ref), (t_ref, to_ref)):
        for start in range(0, rows, 8):
            x = ref[:, 0, start : start + 8, :].reshape(channels * 8, columns)
            high, low = halves(x)
            mixed = dot(w_ref[...], jnp.concatenate([high, low], axis=0))
            mixed = mixed[: channels * 8] + mixed[channels * 8 :]
            out[:, start : start + 8, :] = mixed.reshape(channels, 8, columns)


def local_mix(field, tangent, weight, cycle):
    channels, _, z_local, phi_local = field.shape
    rows = 32
    out = jax.ShapeDtypeStruct((channels, z_local, phi_local), f32)
    block = pl.BlockSpec((channels, 1, rows, phi_local), lambda z: (0, cycle, z, 0))
    out_block = pl.BlockSpec((channels, rows, phi_local), lambda z: (0, z, 0))
    size = channels * z_local * phi_local
    return pl.pallas_call(
        local_kernel,
        grid=(z_local // rows,),
        in_specs=[block, block, pl.BlockSpec(weight.shape, lambda z: (0, 0))],
        out_specs=[out_block, out_block],
        out_shape=[out, out],
        compiler_params=pltpu.CompilerParams(vmem_limit_bytes=VMEM_LIMIT),
        cost_estimate=pl.CostEstimate(flops=1024 * size, bytes_accessed=16 * size, transcendentals=0),
        name="local_mix",
    )(field, tangent, weight)


def mix_kernel(s_ref, wr_ref, wi_ref, out_ref):
    channels = s_ref.shape[0]
    lanes = s_ref.shape[-1]
    total = jnp.zeros(out_ref.shape, f32)
    for c in range(channels):
        s = s_ref[c]
        turned = jnp.concatenate([s[..., lanes // 2 :], s[..., : lanes // 2]], axis=-1)
        total = total + s[None] * wr_ref[c][:, None] + turned[None] * wi_ref[c][:, None]
    out_ref[...] = total


def mix(spectrum, wr, wi):
    return pl.pallas_call(
        mix_kernel,
        out_shape=jax.ShapeDtypeStruct((wr.shape[1],) + spectrum.shape[1:], f32),
        compiler_params=pltpu.CompilerParams(vmem_limit_bytes=VMEM_LIMIT),
        name="mode_mix",
    )(spectrum, wr, wi)


def gelu_pair(x, t):
    a = math.sqrt(2.0 / math.pi)
    b = a * 0.044715
    square = x * x
    th = jnp.tanh(x * (a + b * square))
    half = 0.5 * x
    slope = 0.5 + 0.5 * th + half * (1.0 - th * th) * (a + (3.0 * b) * square)
    return half + half * th, slope * t


def inverse_kernel(own_ref, got_ref, bias_ref, phi_ref, z_ref, *refs, n_phi, width):
    cycles = (len(refs) - 2) // 2
    lx, lt = refs[:cycles], refs[cycles : 2 * cycles]
    out_ref, out_t_ref = refs[2 * cycles :]
    groups, _, lanes = own_ref.shape[-3:]
    modes = z_ref.shape[1] // 6
    phi_local = phi_ref.shape[1] // 2
    bias = bias_ref[pl.program_id(0)]
    spectral = []
    for group in range(groups):
        items = [
            (own_ref if slot % 2 == 0 else got_ref)[slot // 2, ..., 0, group, :, :].reshape(modes, lanes)
            for slot in range(n_phi)
        ]
        g = jnp.concatenate(exchange(items, width), axis=0)
        g_high, g_low = halves(g)
        h = dot(jnp.concatenate([g_high, g_low, g_high], axis=1), phi_ref[...])
        for b in range(n_phi):
            part = h[b * modes : (b + 1) * modes]
            part = jnp.concatenate([part[:, :phi_local], part[:, phi_local:]], axis=0)
            spectral.append(halves(part))
    for r in range(cycles):
        values = []
        for high, low in (spectral[r], spectral[cycles + r]):
            values.append(dot(z_ref[...], jnp.concatenate([high, high, low], axis=0)))
        x = values[0] + (lx[r][0] + bias)
        t = values[1] + lt[r][0]
        out, out_t = gelu_pair(x, t)
        out_ref[0, r] = out
        out_t_ref[0, r] = out_t


def inverse(own, got, bias, phi_table, z_table, local_x, local_t, n_phi, width):
    channels, z_local, phi_local = local_x[0].shape
    cycles = len(local_x)
    lead = own.shape[:-4]
    block = pl.BlockSpec(lead + (1,) + own.shape[-3:], lambda o: (0,) * len(lead) + (o, 0, 0, 0))
    local_block = pl.BlockSpec((1, z_local, phi_local), lambda o: (o, 0, 0))
    out = jax.ShapeDtypeStruct((channels, cycles, z_local, phi_local), f32)
    out_block = pl.BlockSpec((1, cycles, z_local, phi_local), lambda o: (o, 0, 0, 0))
    size = channels * cycles * z_local * phi_local
    return pl.pallas_call(
        functools.partial(inverse_kernel, n_phi=n_phi, width=width),
        grid=(channels,),
        in_specs=[
            block,
            block,
            pl.BlockSpec(memory_space=pltpu.SMEM),
            pl.BlockSpec(phi_table.shape, lambda o: (0, 0)),
            pl.BlockSpec(z_table.shape, lambda o: (0, 0)),
        ]
        + [local_block] * (2 * cycles),
        out_specs=[out_block, out_block],
        out_shape=[out, out],
        compiler_params=pltpu.CompilerParams(vmem_limit_bytes=VMEM_LIMIT),
        cost_estimate=pl.CostEstimate(
            flops=1600 * size, bytes_accessed=16 * size, transcendentals=size
        ),
        name="inverse_transform",
    )(own, got, bias, phi_table, z_table, *local_x, *local_t)


def swap(x, axis, bit):
    count = lax.axis_size(axis)
    return lax.ppermute(x, axis, [(i, i ^ bit) for i in range(count)])


def reduce_scatter(keep, send, n_phi, n_gz):
    got = swap(send, "phi", 1)
    half = keep.shape[2] // 2
    total = keep + got
    a, b = total[:, :, :half], total[:, :, half:]
    a_got = swap(a[1], "phi", 2)
    b_got = swap(b[:, n_gz // 2 :], "gz", 1)
    a = a[0] + a_got
    b = b[:, : n_gz // 2] + b_got
    a_got = swap(a[n_gz // 2 :], "gz", 1)
    b_got = swap(b[1], "phi", 2)
    a = a[: n_gz // 2] + a_got
    b = b[0] + b_got
    v = jnp.concatenate([a, b], axis=1)
    bit = 2
    while bit < n_gz:
        middle = v.shape[0] // 2
        v = v[:middle] + swap(v[middle:], "gz", bit)
        bit *= 2
    return v[0]


def all_gather(v, n_phi, n_gz):
    v = v[None]
    bit = n_gz // 2
    while bit > 1:
        v = jnp.concatenate([v, swap(v, "gz", bit)], axis=0)
        bit //= 2
    half = v.shape[1] // 2
    a, b = v[None, :, :half], v[None, :, half:]
    a_got = swap(a, "gz", 1)
    b_got = swap(b, "phi", 2)
    a = jnp.concatenate([a, a_got], axis=1)
    b = jnp.concatenate([b, b_got], axis=0)
    a_got = swap(a, "phi", 2)
    b_got = swap(b, "gz", 1)
    a = jnp.concatenate([a, a_got], axis=0)
    b = jnp.concatenate([b, b_got], axis=1)
    own = jnp.concatenate([a, b], axis=2)
    return own, swap(own, "phi", 1)


def gz_order(n_gz):
    bits = n_gz.bit_length() - 1
    return [
        sum(digit << i for i, digit in enumerate(digits))
        for digits in itertools.product((0, 1), repeat=bits)
    ]


def body(field, field_tangent, spectral_weight, local_weight, bias_term, z_modes, phi_modes):
    channels, cycles, z_local, phi_local = field.shape
    n_gz = lax.axis_size("gz")
    n_phi = lax.axis_size("phi")
    z_total = z_local * n_gz
    phi_total = phi_local * n_phi
    kz = z_modes.shape[0]
    kp = phi_modes.shape[0]
    width = kp // n_phi
    my_gz = lax.axis_index("gz")
    my_phi = lax.axis_index("phi")

    z_global = my_gz * z_local + jnp.arange(z_local, dtype=jnp.int32)
    phi_global = my_phi * phi_local + jnp.arange(phi_local, dtype=jnp.int32)
    z_kept = z_modes.reshape(n_gz, -1)[my_gz ^ jnp.array(gz_order(n_gz), jnp.int32)].reshape(-1)
    phi_kept = phi_modes.reshape(n_phi, -1)[my_phi ^ jnp.arange(n_phi, dtype=jnp.int32)].reshape(-1)
    zc, zs = angles(z_global, z_kept, z_total)
    pc, ps = angles(phi_global, phi_kept, phi_total)

    high, low = split(jnp.concatenate([pc, -ps], axis=1))
    phi_table = jnp.concatenate(
        [jnp.concatenate([high, low], 1), jnp.concatenate([high, jnp.zeros_like(low)], 1)], 0
    )
    high, low = split(jnp.concatenate([zc, zs], axis=1).T)
    z_table = jnp.concatenate([high, low], 0)
    high, low = split(jnp.concatenate([zc, -zs], axis=1))
    z_back = jnp.concatenate([high, low, high], 1)
    high, low = split(
        jnp.concatenate(
            [jnp.concatenate([pc.T, ps.T], 1), jnp.concatenate([-ps.T, pc.T], 1)], 0
        )
    )
    phi_back = jnp.concatenate([high, high, low], 0)

    high, low = split(jnp.kron(local_weight.T, jnp.eye(8, dtype=f32)))
    local_table = jnp.concatenate(
        [jnp.concatenate([high, high], 1), jnp.concatenate([low, low], 1)], 0
    )

    scale = (1.0 / math.sqrt(z_total * phi_total)) * (2.0 / math.sqrt(kz * kp))
    spread = jnp.tile(jnp.eye(width, dtype=f32), (1, 2 * n_phi)) * scale
    sign = jnp.where(jnp.arange(2 * kp) < kp, -1.0, 1.0).astype(f32)
    wide = jnp.dot(spectral_weight, spread, precision=lax.Precision.HIGHEST)
    wr, wi = wide[0], wide[1] * sign

    keep, send = forward(field, field_tangent, phi_table, z_table, n_phi, n_gz, width)
    spectrum = reduce_scatter(keep, send, n_phi, n_gz)
    local = [local_mix(field, field_tangent, local_table, r) for r in range(cycles)]
    mixed = mix(spectrum, wr, wi)
    own, got = all_gather(mixed, n_phi, n_gz)
    return inverse(
        own,
        got,
        bias_term,
        phi_back,
        z_back,
        [x for x, _ in local],
        [t for _, t in local],
        n_phi,
        width,
    )


def solution(mesh):
    return jax.shard_map(
        body,
        mesh=mesh,
        in_specs=(
            P(None, None, "gz", "phi"),
            P(None, None, "gz", "phi"),
            P(None, None, None, "gz", "phi"),
            P(),
            P(),
            P(),
            P(),
        ),
        out_specs=(P(None, None, "gz", "phi"), P(None, None, "gz", "phi")),
        check_vma=False,
    )
```

```python
import functools
import itertools
import math

import jax
import jax.numpy as jnp
from jax import lax
from jax.experimental import pallas as pl
from jax.experimental.pallas import tpu as pltpu
from jax.sharding import PartitionSpec as P

f32 = jnp.float32
bf16 = jnp.bfloat16
VMEM_LIMIT = 56 * 1024 * 1024


def split(x):
    high = lax.reduce_precision(x, 8, 7)
    return high.astype(bf16), (x - high).astype(bf16)


def halves(x):
    high = x.astype(bf16)
    return high, (x - high.astype(f32)).astype(bf16)


def dot(a, b):
    return lax.dot_general(a, b, (((1,), (0,)), ((), ())), preferred_element_type=f32)


def angles(positions, modes, length):
    product = positions[:, None] * modes[None, :] % length
    angle = product.astype(f32) * (2.0 * math.pi / length)
    return jnp.cos(angle), jnp.sin(angle)


def exchange(items, width):
    items = list(items)
    count = len(items)
    lanes = items[0].shape[-1]
    lane = lax.broadcasted_iota(jnp.int32, items[0].shape, items[0].ndim - 1)
    step = 1
    while step < count:
        shift = width * step
        low = (lane // shift) % 2 == 0
        for i in range(count):
            if i & step:
                continue
            a, b = items[i], items[i | step]
            items[i] = jnp.where(low, a, pltpu.roll(b, shift, 1))
            items[i | step] = jnp.where(low, pltpu.roll(a, lanes - shift, 1), b)
        step *= 2
    return items


def forward_kernel(x_ref, t_ref, phi_ref, z_ref, keep_ref, send_ref, *, n_phi, width):
    block, cycles, z_local, phi_local = x_ref.shape
    modes2 = z_ref.shape[0] // 2
    modes = modes2 // 2
    lanes = phi_ref.shape[1] // 2
    shape = keep_ref.shape[1:-4] + keep_ref.shape[-2:]
    lane = lax.broadcasted_iota(jnp.int32, (modes, lanes), 1)
    sign = jnp.where(lane < lanes // 2, 1.0, -1.0).astype(f32)

    def along_phi(c, part):
        x = (x_ref, t_ref)[part][c].reshape(cycles * z_local, phi_local)
        high, low = halves(x)
        y = dot(jnp.concatenate([high, low], axis=1), phi_ref[...])
        high, low = halves(y[:, :lanes] + y[:, lanes:])
        return jnp.concatenate([high, low], axis=1)

    def along_z(y):
        return [dot(z_ref[...], y[r * z_local : (r + 1) * z_local]) for r in range(cycles)]

    def finish(c, products):
        items = []
        for m in products:
            m = m[:modes2, :lanes] + (m[:modes2, lanes:] + m[modes2:, :lanes])
            items.append(m[:modes] + sign * pltpu.roll(m[modes:], lanes // 2, 1))
        for group in range(len(items) // n_phi):
            part = exchange(items[group * n_phi : (group + 1) * n_phi], width)
            for slot, item in enumerate(part):
                out = keep_ref if slot % 2 == 0 else send_ref
                out[slot // 2, ..., c, group, :, :] = item.reshape(shape)

    steps = [(c, part) for c in range(block) for part in range(2)]
    ahead = along_phi(*steps[0])
    products = []
    for i, (c, part) in enumerate(steps):
        y = ahead
        if i + 1 < len(steps):
            ahead = along_phi(*steps[i + 1])
        products.append(along_z(y))
        if part == 0 and c:
            finish(c - 1, products[-3] + products[-2])
    finish(block - 1, products[-2] + products[-1])


def forward(field, tangent, phi_table, z_table, n_phi, n_gz, width):
    channels, cycles, z_local, phi_local = field.shape
    groups = 2 * cycles // n_phi
    modes = z_table.shape[0] // 4
    lanes = phi_table.shape[1] // 2
    out = jax.ShapeDtypeStruct((n_phi // 2, n_gz, channels, groups, modes // n_gz, lanes), f32)
    step = 4
    block = pl.BlockSpec((step, cycles, z_local, phi_local), lambda c: (c, 0, 0, 0))
    out_block = pl.BlockSpec(
        (n_phi // 2, n_gz, step, groups, modes // n_gz, lanes), lambda c: (0, 0, c, 0, 0, 0)
    )
    return pl.pallas_call(
        functools.partial(forward_kernel, n_phi=n_phi, width=width),
        grid=(channels // step,),
        in_specs=[
            block,
            block,
            pl.BlockSpec(phi_table.shape, lambda c: (0, 0)),
            pl.BlockSpec(z_table.shape, lambda c: (0, 0)),
        ],
        out_specs=[out_block, out_block],
        out_shape=[out, out],
        compiler_params=pltpu.CompilerParams(vmem_limit_bytes=VMEM_LIMIT),
        cost_estimate=pl.CostEstimate(
            flops=12 * field.size * phi_table.shape[1],
            bytes_accessed=8 * field.size,
            transcendentals=0,
        ),
        name="forward_transform",
    )(field, tangent, phi_table, z_table)


def local_kernel(x_ref, t_ref, w_ref, xo_ref, to_ref):
    channels, _, rows, columns = x_ref.shape
    tiles = [
        (ref, out, start) for ref, out in ((x_ref, xo_ref), (t_ref, to_ref)) for start in range(0, rows, 8)
    ]
    for at in range(0, len(tiles), 4):
        products = []
        for ref, _, start in tiles[at : at + 4]:
            high, low = halves(ref[:, 0, start : start + 8, :].reshape(channels * 8, columns))
            products.append(dot(w_ref[...], jnp.concatenate([high, low], axis=0)))
        for (_, out, start), m in zip(tiles[at : at + 4], products):
            m = m[: channels * 8] + m[channels * 8 :]
            out[:, start : start + 8, :] = m.reshape(channels, 8, columns)


def local_mix(field, tangent, weight, cycle, part, parts):
    channels, _, z_local, phi_local = field.shape
    span = z_local // parts
    rows = min(64, span)
    steps = span // rows
    out = jax.ShapeDtypeStruct((channels, span, phi_local), f32)
    block = pl.BlockSpec((channels, 1, rows, phi_local), lambda z: (0, cycle, part * steps + z, 0))
    out_block = pl.BlockSpec((channels, rows, phi_local), lambda z: (0, z, 0))
    size = channels * span * phi_local
    return pl.pallas_call(
        local_kernel,
        grid=(steps,),
        in_specs=[block, block, pl.BlockSpec(weight.shape, lambda z: (0, 0))],
        out_specs=[out_block, out_block],
        out_shape=[out, out],
        compiler_params=pltpu.CompilerParams(vmem_limit_bytes=VMEM_LIMIT),
        cost_estimate=pl.CostEstimate(flops=1024 * size, bytes_accessed=16 * size, transcendentals=0),
        name="local_mix",
    )(field, tangent, weight)


def mix_kernel(s_ref, wr_ref, wi_ref, out_ref):
    channels = s_ref.shape[0]
    lanes = s_ref.shape[-1]
    total = jnp.zeros(out_ref.shape, f32)
    for c in range(channels):
        s = s_ref[c]
        turned = jnp.concatenate([s[..., lanes // 2 :], s[..., : lanes // 2]], axis=-1)
        total = total + s[None] * wr_ref[c][:, None] + turned[None] * wi_ref[c][:, None]
    out_ref[...] = total


def mix(spectrum, wr, wi):
    return pl.pallas_call(
        mix_kernel,
        out_shape=jax.ShapeDtypeStruct((wr.shape[1],) + spectrum.shape[1:], f32),
        compiler_params=pltpu.CompilerParams(vmem_limit_bytes=VMEM_LIMIT),
        name="mode_mix",
    )(spectrum, wr, wi)


def gelu_pair(x, t):
    a = math.sqrt(2.0 / math.pi)
    b = a * 0.044715
    square = x * x
    th = jnp.tanh(x * (a + b * square))
    half = 0.5 * x
    slope = 0.5 + 0.5 * th + half * (1.0 - th * th) * (a + (3.0 * b) * square)
    return half + half * th, slope * t


def inverse_kernel(own_ref, got_ref, bias_ref, phi_ref, z_ref, *refs, n_phi, width):
    out_ref, out_t_ref = refs[-2:]
    block, cycles, z_local, phi_local = out_ref.shape
    parts = (len(refs) - 2) // (2 * cycles)
    span = z_local // parts
    groups, _, lanes = own_ref.shape[-3:]
    modes = z_ref.shape[1] // 6
    for c in range(block):
        bias = bias_ref[pl.program_id(0) * block + c]
        spectral = []
        for group in range(groups):
            items = [
                (own_ref if slot % 2 == 0 else got_ref)[slot // 2, ..., c, group, :, :].reshape(modes, lanes)
                for slot in range(n_phi)
            ]
            high, low = halves(jnp.concatenate(exchange(items, width), axis=0))
            h = dot(jnp.concatenate([high, low, high], axis=1), phi_ref[...])
            for b in range(n_phi):
                part = h[b * modes : (b + 1) * modes]
                part = jnp.concatenate([part[:, :phi_local], part[:, phi_local:]], axis=0)
                high, low = halves(part)
                spectral.append(jnp.concatenate([high, high, low], axis=0))
        values = [dot(z_ref[...], part) for part in spectral]
        for r in range(cycles):
            for p in range(parts):
                rows = slice(p * span, (p + 1) * span)
                lx, lt = refs[2 * (r * parts + p) : 2 * (r * parts + p) + 2]
                x = values[r][rows] + (lx[c] + bias)
                t = values[cycles + r][rows] + lt[c]
                out_ref[c, r, rows], out_t_ref[c, r, rows] = gelu_pair(x, t)


def inverse(own, got, bias, phi_table, z_table, local, cycles, n_phi, width):
    channels, span, phi_local = local[0].shape
    z_local = span * len(local) // (2 * cycles)
    lead = own.shape[:-4]
    step = 2
    block = pl.BlockSpec(lead + (step,) + own.shape[-3:], lambda o: (0,) * len(lead) + (o, 0, 0, 0))
    local_block = pl.BlockSpec((step, span, phi_local), lambda o: (o, 0, 0))
    out = jax.ShapeDtypeStruct((channels, cycles, z_local, phi_local), f32)
    out_block = pl.BlockSpec((step, cycles, z_local, phi_local), lambda o: (o, 0, 0, 0))
    size = channels * cycles * z_local * phi_local
    return pl.pallas_call(
        functools.partial(inverse_kernel, n_phi=n_phi, width=width),
        grid=(channels // step,),
        in_specs=[
            block,
            block,
            pl.BlockSpec(memory_space=pltpu.SMEM),
            pl.BlockSpec(phi_table.shape, lambda o: (0, 0)),
            pl.BlockSpec(z_table.shape, lambda o: (0, 0)),
        ]
        + [local_block] * len(local),
        out_specs=[out_block, out_block],
        out_shape=[out, out],
        compiler_params=pltpu.CompilerParams(vmem_limit_bytes=VMEM_LIMIT),
        cost_estimate=pl.CostEstimate(
            flops=1600 * size, bytes_accessed=16 * size, transcendentals=size
        ),
        name="inverse_transform",
    )(own, got, bias, phi_table, z_table, *local)


def swap(x, axis, bit):
    count = lax.axis_size(axis)
    return lax.ppermute(x, axis, [(i, i ^ bit) for i in range(count)])


class Filler:
    def __init__(self, field, tangent, table, parts):
        self.inputs = (field, tangent)
        self.table = table
        self.parts = parts
        self.todo = [(r, p) for r in range(field.shape[1]) for p in range(parts)]
        self.done = []

    def beside(self, sent, got, count=1):
        for _ in range(min(count, len(self.todo))):
            r, p = self.todo.pop(0)
            inputs, _ = lax.optimization_barrier((self.inputs, sent))
            piece = local_mix(*inputs, self.table, r, p, self.parts)
            got, piece = lax.optimization_barrier((got, piece))
            self.done += piece
        return got


def reduce_scatter(keep, send, n_phi, n_gz, filler):
    got = swap(send, "phi", 1)
    half = keep.shape[2] // 2
    total = keep + got
    a, b = total[:, :, :half], total[:, :, half:]
    sent = (a[1], b[:, n_gz // 2 :])
    got = (swap(sent[0], "phi", 2), swap(sent[1], "gz", 1))
    a_got, b_got = filler.beside(sent, got, 2)
    a = a[0] + a_got
    b = b[:, : n_gz // 2] + b_got
    sent = (a[n_gz // 2 :], b[1])
    got = (swap(sent[0], "gz", 1), swap(sent[1], "phi", 2))
    a_got, b_got = filler.beside(sent, got)
    a = a[: n_gz // 2] + a_got
    b = b[0] + b_got
    v = jnp.concatenate([a, b], axis=1)
    bit = 2
    while bit < n_gz:
        middle = v.shape[0] // 2
        sent = v[middle:]
        v = v[:middle] + filler.beside(sent, swap(sent, "gz", bit))
        bit *= 2
    return v[0]


def all_gather(v, n_phi, n_gz, filler):
    v = v[None]
    bit = n_gz // 2
    while bit > 1:
        v = jnp.concatenate([v, filler.beside(v, swap(v, "gz", bit))], axis=0)
        bit //= 2
    half = v.shape[1] // 2
    a, b = v[None, :, :half], v[None, :, half:]
    got = (swap(a, "gz", 1), swap(b, "phi", 2))
    a_got, b_got = filler.beside((a, b), got)
    a = jnp.concatenate([a, a_got], axis=1)
    b = jnp.concatenate([b, b_got], axis=0)
    got = (swap(a, "phi", 2), swap(b, "gz", 1))
    a_got, b_got = filler.beside((a, b), got, len(filler.todo))
    a = jnp.concatenate([a, a_got], axis=0)
    b = jnp.concatenate([b, b_got], axis=1)
    own = jnp.concatenate([a, b], axis=2)
    return own, swap(own, "phi", 1)


def gz_order(n_gz):
    bits = n_gz.bit_length() - 1
    return [
        sum(digit << i for i, digit in enumerate(digits))
        for digits in itertools.product((0, 1), repeat=bits)
    ]


def body(field, field_tangent, spectral_weight, local_weight, bias_term, z_modes, phi_modes):
    channels, cycles, z_local, phi_local = field.shape
    n_gz = lax.axis_size("gz")
    n_phi = lax.axis_size("phi")
    z_total = z_local * n_gz
    phi_total = phi_local * n_phi
    kz = z_modes.shape[0]
    kp = phi_modes.shape[0]
    width = kp // n_phi
    my_gz = lax.axis_index("gz")
    my_phi = lax.axis_index("phi")

    z_global = my_gz * z_local + jnp.arange(z_local, dtype=jnp.int32)
    phi_global = my_phi * phi_local + jnp.arange(phi_local, dtype=jnp.int32)
    z_kept = z_modes.reshape(n_gz, -1)[my_gz ^ jnp.array(gz_order(n_gz), jnp.int32)].reshape(-1)
    phi_kept = phi_modes.reshape(n_phi, -1)[my_phi ^ jnp.arange(n_phi, dtype=jnp.int32)].reshape(-1)
    zc, zs = angles(z_global, z_kept, z_total)
    pc, ps = angles(phi_global, phi_kept, phi_total)

    high, low = split(jnp.concatenate([pc, -ps], axis=1))
    phi_table = jnp.concatenate(
        [jnp.concatenate([high, low], 1), jnp.concatenate([high, jnp.zeros_like(low)], 1)], 0
    )
    high, low = split(jnp.concatenate([zc, zs], axis=1).T)
    z_table = jnp.concatenate([high, low], 0)
    high, low = split(jnp.concatenate([zc, -zs], axis=1))
    z_back = jnp.concatenate([high, low, high], 1)
    high, low = split(
        jnp.concatenate(
            [jnp.concatenate([pc.T, ps.T], 1), jnp.concatenate([-ps.T, pc.T], 1)], 0
        )
    )
    phi_back = jnp.concatenate([high, high, low], 0)

    high, low = split(jnp.kron(local_weight.T, jnp.eye(8, dtype=f32)))
    local_table = jnp.concatenate(
        [jnp.concatenate([high, high], 1), jnp.concatenate([low, low], 1)], 0
    )

    scale = (1.0 / math.sqrt(z_total * phi_total)) * (2.0 / math.sqrt(kz * kp))
    spread = jnp.tile(jnp.eye(width, dtype=f32), (1, 2 * n_phi)) * scale
    sign = jnp.where(jnp.arange(2 * kp) < kp, -1.0, 1.0).astype(f32)
    wide = jnp.dot(spectral_weight, spread, precision=lax.Precision.HIGHEST)
    wr, wi = wide[0], wide[1] * sign

    keep, send = forward(field, field_tangent, phi_table, z_table, n_phi, n_gz, width)
    filler = Filler(field, field_tangent, local_table, 2)
    spectrum = reduce_scatter(keep, send, n_phi, n_gz, filler)
    mixed = mix(spectrum, wr, wi)
    own, got = all_gather(mixed, n_phi, n_gz, filler)
    return inverse(own, got, bias_term, phi_back, z_back, filler.done, cycles, n_phi, width)


def solution(mesh):
    return jax.shard_map(
        body,
        mesh=mesh,
        in_specs=(
            P(None, None, "gz", "phi"),
            P(None, None, "gz", "phi"),
            P(None, None, None, "gz", "phi"),
            P(),
            P(),
            P(),
            P(),
        ),
        out_specs=(P(None, None, "gz", "phi"), P(None, None, "gz", "phi")),
        check_vma=False,
    )
```

```python
import functools
import itertools
import math

import jax
import jax.numpy as jnp
from jax import lax
from jax.experimental import pallas as pl
from jax.experimental.pallas import tpu as pltpu
from jax.sharding import PartitionSpec as P

f32 = jnp.float32
bf16 = jnp.bfloat16
MIB = 1024 * 1024


def split(x):
    high = lax.reduce_precision(x, 8, 7)
    return high.astype(bf16), (x - high).astype(bf16)


def halves(x):
    high = x.astype(bf16)
    return high, (x - high.astype(f32)).astype(bf16)


def dot(a, b):
    return lax.dot_general(a, b, (((1,), (0,)), ((), ())), preferred_element_type=f32)


def angles(positions, modes, length):
    product = positions[:, None] * modes[None, :] % length
    angle = product.astype(f32) * (2.0 * math.pi / length)
    return jnp.cos(angle), jnp.sin(angle)


def exchange(items, width):
    items = list(items)
    count = len(items)
    lanes = items[0].shape[-1]
    lane = lax.broadcasted_iota(jnp.int32, items[0].shape, items[0].ndim - 1)
    step = 1
    while step < count:
        shift = width * step
        low = (lane // shift) % 2 == 0
        for i in range(count):
            if i & step:
                continue
            a, b = items[i], items[i | step]
            items[i] = jnp.where(low, a, pltpu.roll(b, shift, 1))
            items[i | step] = jnp.where(low, pltpu.roll(a, lanes - shift, 1), b)
        step *= 2
    return items


def wrap(x, n):
    return x & (n - 1) if n & (n - 1) == 0 else lax.rem(x, n)


def cosines(turns, n):
    return jnp.cos(wrap(turns, n).astype(f32) * (2.0 * math.pi / n))


def build_tables(z_modes, phi_modes, phi_ref, z_ref, n_gz, n_phi):
    phi_local, lanes = phi_ref.shape[0] // 2, phi_ref.shape[1] // 2
    rows, z_local = z_ref.shape[0] // 2, z_ref.shape[1]
    kp, kz = lanes // 2, rows // 2
    width, depth = kp // n_phi, kz // n_gz
    n = n_phi * phi_local
    me = lax.axis_index("phi")
    lane = lax.broadcasted_iota(jnp.int32, (8, lanes), 1)
    mode = jnp.zeros((8, lanes), jnp.int32)
    for i in range(kp):
        value = phi_modes[((i // width) ^ me) * width + i % width]
        mode = jnp.where((lane == i) | (lane == i + kp), value, mode)
    quarter = jnp.where(lane < kp, 0, n // 4)
    position = me * phi_local + lax.broadcasted_iota(jnp.int32, (phi_local, lanes), 0)
    high, low = halves(cosines(position * mode[:1] + quarter[:1], n))
    phi_ref[:phi_local, :lanes] = high
    phi_ref[:phi_local, lanes:] = low
    phi_ref[phi_local:, :lanes] = high
    phi_ref[phi_local:, lanes:] = jnp.zeros_like(low)

    n = n_gz * z_local
    me = lax.axis_index("gz")
    order = gz_order(n_gz)
    row = lax.broadcasted_iota(jnp.int32, (kz, z_local), 0)
    mode = jnp.zeros((kz, z_local), jnp.int32)
    for i in range(kz):
        value = z_modes[(order[i // depth] ^ me) * depth + i % depth]
        mode = jnp.where(row == i, value, mode)
    position = me * z_local + lax.broadcasted_iota(jnp.int32, (kz, z_local), 1)
    turns = position * mode
    for part, quarter in enumerate((0, 3 * n // 4)):
        high, low = halves(cosines(turns + quarter, n))
        z_ref[part * kz : (part + 1) * kz] = high
        z_ref[rows + part * kz : rows + (part + 1) * kz] = low


def forward_kernel(
    z_modes, phi_modes, x_ref, t_ref, ak_ref, as_ref, bk_ref, bs_ref, phi_ref, z_ref, *, n_gz, n_phi
):
    at, count = pl.program_id(0), pl.num_programs(0)

    @pl.when(at == 0)
    def _():
        build_tables(z_modes, phi_modes, phi_ref, z_ref, n_gz, n_phi)

    width = phi_ref.shape[1] // (4 * n_phi)
    for first, keep_ref, send_ref in ((True, ak_ref, as_ref), (False, bk_ref, bs_ref)):

        @pl.when((at < count // 2) == first)
        def _():
            transform(phi_ref, z_ref, x_ref, t_ref, keep_ref, send_ref, n_phi, width)


def transform(phi_ref, z_ref, x_ref, t_ref, keep_ref, send_ref, n_phi, width):
    block, cycles, z_local, phi_local = x_ref.shape
    modes2 = z_ref.shape[0] // 2
    modes = modes2 // 2
    lanes = phi_ref.shape[1] // 2
    shape = keep_ref.shape[1:-4] + keep_ref.shape[-2:]
    lane = lax.broadcasted_iota(jnp.int32, (modes, lanes), 1)
    sign = jnp.where(lane < lanes // 2, 1.0, -1.0).astype(f32)

    def along_phi(c, part):
        x = (x_ref, t_ref)[part][c].reshape(cycles * z_local, phi_local)
        high, low = halves(x)
        y = dot(jnp.concatenate([high, low], axis=1), phi_ref[...])
        high, low = halves(y[:, :lanes] + y[:, lanes:])
        return jnp.concatenate([high, low], axis=1)

    def along_z(y):
        return [dot(z_ref[...], y[r * z_local : (r + 1) * z_local]) for r in range(cycles)]

    def finish(c, products):
        items = []
        for m in products:
            m = m[:modes2, :lanes] + (m[:modes2, lanes:] + m[modes2:, :lanes])
            items.append(m[:modes] + sign * pltpu.roll(m[modes:], lanes // 2, 1))
        for group in range(len(items) // n_phi):
            part = exchange(items[group * n_phi : (group + 1) * n_phi], width)
            for slot, item in enumerate(part):
                out = keep_ref if slot % 2 == 0 else send_ref
                out[slot // 2, ..., c, group, :, :] = item.reshape(shape)

    steps = [(c, part) for c in range(block) for part in range(2)]
    ahead = along_phi(*steps[0])
    products = []
    for i, (c, part) in enumerate(steps):
        y = ahead
        if i + 1 < len(steps):
            ahead = along_phi(*steps[i + 1])
        products.append(along_z(y))
        if part == 0 and c:
            finish(c - 1, products[-3] + products[-2])
    finish(block - 1, products[-2] + products[-1])


def forward(field, tangent, z_modes, phi_modes, n_phi, n_gz):
    channels, cycles, z_local, phi_local = field.shape
    groups = 2 * cycles // n_phi
    kz, kp = z_modes.shape[0], phi_modes.shape[0]
    lanes = 2 * kp
    out = jax.ShapeDtypeStruct((n_phi // 2, n_gz, channels // 2, groups, kz // n_gz, lanes), f32)
    step = 4
    steps = channels // step
    block = pl.BlockSpec((step, cycles, z_local, phi_local), lambda c: (c, 0, 0, 0))
    shape = (n_phi // 2, n_gz, step, groups, kz // n_gz, lanes)
    a_block = pl.BlockSpec(shape, lambda c: (0, 0, jnp.minimum(c, steps // 2 - 1), 0, 0, 0))
    b_block = pl.BlockSpec(shape, lambda c: (0, 0, jnp.maximum(c - steps // 2, 0), 0, 0, 0))
    return pl.pallas_call(
        functools.partial(forward_kernel, n_gz=n_gz, n_phi=n_phi),
        grid=(steps,),
        in_specs=[pl.BlockSpec(memory_space=pltpu.SMEM)] * 2 + [block, block],
        out_specs=[a_block, a_block, b_block, b_block],
        out_shape=[out] * 4,
        scratch_shapes=[
            pltpu.VMEM((2 * phi_local, 2 * lanes), bf16),
            pltpu.VMEM((4 * kz, z_local), bf16),
        ],
        compiler_params=pltpu.CompilerParams(vmem_limit_bytes=36 * MIB),
        cost_estimate=pl.CostEstimate(
            flops=24 * field.size * lanes, bytes_accessed=8 * field.size, transcendentals=0
        ),
        name="forward_transform",
    )(z_modes, phi_modes, field, tangent)


def local_kernel(x_ref, t_ref, w_ref, bias_ref, xo_ref, to_ref):
    channels, _, rows, columns = x_ref.shape
    base = pl.multiple_of(pl.program_id(0) * rows, rows)
    tiles = [
        (ref, out, start) for ref, out in ((x_ref, xo_ref), (t_ref, to_ref)) for start in range(0, rows, 8)
    ]
    for at in range(0, len(tiles), 4):
        products = []
        for ref, _, start in tiles[at : at + 4]:
            high, low = halves(ref[:, 0, start : start + 8, :].reshape(channels * 8, columns))
            products.append(dot(w_ref[...], jnp.concatenate([high, low], axis=0)))
        for (_, out, start), m in zip(tiles[at : at + 4], products):
            m = (m[: channels * 8] + m[channels * 8 :]).reshape(channels, 8, columns)
            out[:, pl.ds(base + start, 8), :] = m + bias_ref[...] if out is xo_ref else m


def local_mix(field, tangent, weight, bias, cycle, part, parts):
    channels, _, z_local, phi_local = field.shape
    span = z_local // parts
    rows = min(64, span)
    steps = span // rows
    out = pltpu.VMEM((channels, span, phi_local), f32)
    block = pl.BlockSpec((channels, 1, rows, phi_local), lambda z: (0, cycle, part * steps + z, 0))
    out_block = pl.BlockSpec(memory_space=pltpu.VMEM)
    size = channels * span * phi_local
    return pl.pallas_call(
        local_kernel,
        grid=(steps,),
        in_specs=[
            block,
            block,
            pl.BlockSpec(weight.shape, lambda z: (0, 0)),
            pl.BlockSpec(bias.shape, lambda z: (0, 0, 0)),
        ],
        out_specs=[out_block, out_block],
        out_shape=[out, out],
        compiler_params=pltpu.CompilerParams(vmem_limit_bytes=16 * MIB),
        cost_estimate=pl.CostEstimate(flops=1024 * size, bytes_accessed=8 * size, transcendentals=0),
        name="local_mix",
    )(field, tangent, weight, bias)


def mix_kernel(s_ref, wr_ref, wi_ref, out_ref):
    channels = s_ref.shape[0]
    lanes = s_ref.shape[-1]
    total = jnp.zeros(out_ref.shape, f32)
    for c in range(channels):
        s = s_ref[c]
        turned = jnp.concatenate([s[..., lanes // 2 :], s[..., : lanes // 2]], axis=-1)
        total = total + s[None] * wr_ref[c][:, None] + turned[None] * wi_ref[c][:, None]
    out_ref[...] = total


def mix(spectrum, wr, wi):
    return pl.pallas_call(
        mix_kernel,
        out_shape=jax.ShapeDtypeStruct((wr.shape[1],) + spectrum.shape[1:], f32),
        compiler_params=pltpu.CompilerParams(vmem_limit_bytes=8 * MIB),
        name="mode_mix",
    )(spectrum, wr, wi)


def gelu_pair(x, t):
    a = math.sqrt(2.0 / math.pi)
    b = a * 0.044715
    square = x * x
    s = 0.5 + 0.5 * jnp.tanh(x * (a + b * square))
    out = x * s
    return out, t * (s + out * ((1.0 - s) * (2.0 * a + (6.0 * b) * square)))


def inverse_kernel(*refs, n_phi, width):
    own, other = refs[:4], refs[4:8]
    phi_ref, z_ref = refs[8:10]
    out_ref, out_t_ref = refs[-2:]
    refs = refs[10:-2]
    block, cycles, z_local, phi_local = out_ref.shape
    parts = len(refs) // (2 * cycles)
    span = z_local // parts
    groups, depth, lanes = own[0].shape[-3:]
    modes = z_ref.shape[1] // 6
    first = pl.program_id(0) < pl.num_programs(0) // 2
    at = pl.program_id(0) * block

    def slots(pieces, c, group):
        v, ab1, a2, b2 = pieces
        ab1 = ab1[:, c, group]
        low = [v[:, c, group], jnp.where(first, ab1, b2[0, :, c, group])]
        high = [
            jnp.where(first, a2[0, :, c, group], ab1),
            jnp.where(first, a2[1, :, c, group], b2[1, :, c, group]),
        ]
        return [jnp.concatenate(rows, axis=0).reshape(modes, lanes) for rows in (low, high)]

    for c in range(block):
        spectral = []
        for group in range(groups):
            pairs = zip(slots(own, c, group), slots(other, c, group))
            items = [item for pair in pairs for item in pair]
            high, low = halves(jnp.concatenate(exchange(items, width), axis=0))
            h = dot(jnp.concatenate([high, low, high], axis=1), phi_ref[...])
            for b in range(n_phi):
                part = h[b * modes : (b + 1) * modes]
                part = jnp.concatenate([part[:, :phi_local], part[:, phi_local:]], axis=0)
                high, low = halves(part)
                spectral.append(jnp.concatenate([high, high, low], axis=0))
        values = [dot(z_ref[...], part) for part in spectral]
        for r in range(cycles):
            for p in range(parts):
                rows = slice(p * span, (p + 1) * span)
                lx, lt = refs[2 * (r * parts + p) : 2 * (r * parts + p) + 2]
                x = values[r][rows] + lx[at + c]
                t = values[cycles + r][rows] + lt[at + c]
                out_ref[c, r, rows], out_t_ref[c, r, rows] = gelu_pair(x, t)


def inverse(own, other, phi_table, z_table, local, cycles, n_phi, width):
    channels, span, phi_local = local[0].shape
    z_local = span * len(local) // (2 * cycles)
    step = 2
    steps = channels // step
    zeros = lambda n: (0,) * n
    shape = (own[0].shape[0], step) + own[0].shape[2:]
    tail = zeros(len(shape) - 2)
    v_block = pl.BlockSpec(shape, lambda o: (0, o) + tail)
    a_block = pl.BlockSpec((2,) + shape, lambda o: (0, 0, jnp.minimum(o, steps // 2 - 1)) + tail)
    b_block = pl.BlockSpec((2,) + shape, lambda o: (0, 0, jnp.maximum(o - steps // 2, 0)) + tail)
    local_block = pl.BlockSpec(memory_space=pltpu.VMEM)
    local = [pltpu.with_memory_space_constraint(piece, pltpu.VMEM) for piece in local]
    out = jax.ShapeDtypeStruct((channels, cycles, z_local, phi_local), f32)
    out_block = pl.BlockSpec((step, cycles, z_local, phi_local), lambda o: (o, 0, 0, 0))
    size = channels * cycles * z_local * phi_local
    return pl.pallas_call(
        functools.partial(inverse_kernel, n_phi=n_phi, width=width),
        grid=(steps,),
        in_specs=[v_block, v_block, a_block, b_block] * 2
        + [
            pl.BlockSpec(phi_table.shape, lambda o: (0, 0)),
            pl.BlockSpec(z_table.shape, lambda o: (0, 0)),
        ]
        + [local_block] * len(local),
        out_specs=[out_block, out_block],
        out_shape=[out, out],
        compiler_params=pltpu.CompilerParams(vmem_limit_bytes=22 * MIB),
        cost_estimate=pl.CostEstimate(
            flops=1600 * size, bytes_accessed=16 * size, transcendentals=size
        ),
        name="inverse_transform",
    )(*own, *other, phi_table, z_table, *local)


def swap(x, axis, bit):
    count = lax.axis_size(axis)
    return lax.ppermute(x, axis, [(i, i ^ bit) for i in range(count)])


class Filler:
    def __init__(self, field, tangent, small, prepare, parts):
        self.inputs = (field, tangent)
        self.small = small
        self.prepare = prepare
        self.tables = None
        self.parts = parts
        self.todo = [(r, p) for r in range(field.shape[1]) for p in range(parts)]
        self.done = []

    def beside(self, sent, got, count=1):
        if self.tables is None:
            small, _ = lax.optimization_barrier((self.small, sent))
            self.tables = self.prepare(*small)
            got, self.tables = lax.optimization_barrier((got, self.tables))
            return got
        for _ in range(min(count, len(self.todo))):
            r, p = self.todo.pop(0)
            inputs, _ = lax.optimization_barrier((self.inputs, sent))
            piece = local_mix(*inputs, *self.tables[:2], r, p, self.parts)
            got, piece = lax.optimization_barrier((got, piece))
            self.done += piece
        return got


def add(terms, *index):
    return functools.reduce(jnp.add, [term[index] for term in terms])


def reduce_scatter(a, b, n_phi, n_gz, filler):
    low, high = slice(n_gz // 2), slice(n_gz // 2, None)
    a = [a[0], swap(a[1], "phi", 1)]
    b = [b[0], swap(b[1], "phi", 1)]
    sent = (add(a, 1), add(b, slice(None), high))
    got = (swap(sent[0], "phi", 2), swap(sent[1], "gz", 1))
    a_got, b_got = filler.beside(sent, got)
    a = [term[0] for term in a] + [a_got]
    b = [term[:, low] for term in b] + [b_got]
    sent = (add(a, high), add(b, 1))
    got = (swap(sent[0], "gz", 1), swap(sent[1], "phi", 2))
    a_got, b_got = filler.beside(sent, got)
    a = [term[low] for term in a] + [a_got]
    b = [term[0] for term in b] + [b_got]
    v = [jnp.concatenate([add(a), add(b)], axis=1)]
    for bits in gz_groups(n_gz):
        count = 1 << len(bits)
        size = v[0].shape[0] // count
        sent = [add(v, slice(i * size, (i + 1) * size)) for i in range(1, count)]
        got = [swap(part, "gz", group_bits(i, bits)) for i, part in enumerate(sent, 1)]
        v = [term[:size] for term in v] + list(filler.beside(sent, got, count // 2))
    return add(v, 0)


def all_gather(v, n_phi, n_gz, filler):
    v = v[None]
    for bits in reversed(gz_groups(n_gz)):
        count = 1 << len(bits)
        got = [swap(v, "gz", group_bits(i, bits)) for i in range(1, count)]
        got = filler.beside(v, got, count // 2)
        v = jnp.concatenate([v, *got], axis=0)
    half = v.shape[1] // 2
    a, b = v[:, :half], v[:, half:]
    got = (swap(a, "gz", 1), swap(b, "phi", 2), swap(v, "phi", 1))
    a1, b1, v_core = filler.beside((a, b), got)
    ab1 = jnp.concatenate([a1, b1], axis=1)
    a, b = jnp.stack([a, a1]), jnp.stack([b, b1])
    got = (swap(a, "phi", 2), swap(b, "gz", 1), swap(ab1, "phi", 1))
    a2, b2, ab1_core = filler.beside((a, b), got, len(filler.todo))
    return (v, ab1, a2, b2), (v_core, ab1_core, swap(a2, "phi", 1), swap(b2, "phi", 1))


def gz_groups(n_gz):
    bits = list(range(1, n_gz.bit_length() - 1))
    return [bits[i : i + 2] for i in range(0, len(bits), 2)]


def group_bits(i, bits):
    digits = [(i >> (len(bits) - 1 - j)) & 1 for j in range(len(bits))]
    return sum(digit << bit for digit, bit in zip(digits, bits))


def gz_order(n_gz):
    bits = n_gz.bit_length() - 1
    return [
        sum(digit << i for i, digit in enumerate(digits))
        for digits in itertools.product((0, 1), repeat=bits)
    ]


def tables(spectral_weight, local_weight, bias_term, z_modes, phi_modes, z_local, phi_local):
    n_gz = lax.axis_size("gz")
    n_phi = lax.axis_size("phi")
    kz, kp = z_modes.shape[0], phi_modes.shape[0]
    width = kp // n_phi
    z_total, phi_total = z_local * n_gz, phi_local * n_phi
    my_gz = lax.axis_index("gz")
    my_phi = lax.axis_index("phi")

    z_global = my_gz * z_local + jnp.arange(z_local, dtype=jnp.int32)
    phi_global = my_phi * phi_local + jnp.arange(phi_local, dtype=jnp.int32)
    z_kept = z_modes.reshape(n_gz, -1)[my_gz ^ jnp.array(gz_order(n_gz), jnp.int32)].reshape(-1)
    phi_kept = phi_modes.reshape(n_phi, -1)[my_phi ^ jnp.arange(n_phi, dtype=jnp.int32)].reshape(-1)
    zc, zs = angles(z_global, z_kept, z_total)
    pc, ps = angles(phi_global, phi_kept, phi_total)
    high, low = split(jnp.concatenate([zc, -zs], axis=1))
    z_back = jnp.concatenate([high, low, high], 1)
    high, low = split(
        jnp.concatenate(
            [jnp.concatenate([pc.T, ps.T], 1), jnp.concatenate([-ps.T, pc.T], 1)], 0
        )
    )
    phi_back = jnp.concatenate([high, high, low], 0)

    high, low = split(jnp.kron(local_weight.T, jnp.eye(8, dtype=f32)))
    local_table = jnp.concatenate(
        [jnp.concatenate([high, high], 1), jnp.concatenate([low, low], 1)], 0
    )
    wide_bias = jnp.broadcast_to(bias_term[:, None, None], (bias_term.shape[0], 8, phi_local))

    scale = (1.0 / math.sqrt(z_total * phi_total)) * (2.0 / math.sqrt(kz * kp))
    spread = jnp.tile(jnp.eye(width, dtype=f32), (1, 2 * n_phi)) * scale
    sign = jnp.where(jnp.arange(2 * kp) < kp, -1.0, 1.0).astype(f32)
    wide = jnp.dot(spectral_weight, spread, precision=lax.Precision.HIGHEST)
    return local_table, wide_bias, phi_back, z_back, wide[0], wide[1] * sign


def body(field, field_tangent, spectral_weight, local_weight, bias_term, z_modes, phi_modes):
    channels, cycles, z_local, phi_local = field.shape
    n_gz = lax.axis_size("gz")
    n_phi = lax.axis_size("phi")
    width = phi_modes.shape[0] // n_phi
    small = (spectral_weight, local_weight, bias_term, z_modes, phi_modes)
    prepare = functools.partial(tables, z_local=z_local, phi_local=phi_local)
    field = pltpu.with_memory_space_constraint(field, pltpu.HBM)
    field_tangent = pltpu.with_memory_space_constraint(field_tangent, pltpu.HBM)
    filler = Filler(field, field_tangent, small, prepare, 2)

    ak, asent, bk, bsent = forward(field, field_tangent, z_modes, phi_modes, n_phi, n_gz)
    spectrum = reduce_scatter((ak, asent), (bk, bsent), n_phi, n_gz, filler)
    _, _, phi_back, z_back, wr, wi = filler.tables
    mixed = mix(spectrum, wr, wi)
    own, other = all_gather(mixed, n_phi, n_gz, filler)
    return inverse(own, other, phi_back, z_back, filler.done, cycles, n_phi, width)


def solution(mesh):
    return jax.shard_map(
        body,
        mesh=mesh,
        in_specs=(
            P(None, None, "gz", "phi"),
            P(None, None, "gz", "phi"),
            P(None, None, None, "gz", "phi"),
            P(),
            P(),
            P(),
            P(),
        ),
        out_specs=(P(None, None, "gz", "phi"), P(None, None, "gz", "phi")),
        check_vma=False,
    )
```

```python
import functools
import itertools
import math

import jax
import jax.numpy as jnp
from jax import lax
from jax.experimental import pallas as pl
from jax.experimental.pallas import tpu as pltpu
from jax.sharding import PartitionSpec as P

f32 = jnp.float32
bf16 = jnp.bfloat16
MIB = 1024 * 1024


def halves(x):
    high = x.astype(bf16)
    return high, (x - high.astype(f32)).astype(bf16)


def dot(a, b):
    return lax.dot_general(a, b, (((1,), (0,)), ((), ())), preferred_element_type=f32)


def exchange(items, width):
    items = list(items)
    count = len(items)
    lanes = items[0].shape[-1]
    lane = lax.broadcasted_iota(jnp.int32, items[0].shape, items[0].ndim - 1)
    step = 1
    while step < count:
        shift = width * step
        low = (lane // shift) % 2 == 0
        for i in range(count):
            if i & step:
                continue
            a, b = items[i], items[i | step]
            items[i] = jnp.where(low, a, pltpu.roll(b, shift, 1))
            items[i | step] = jnp.where(low, pltpu.roll(a, lanes - shift, 1), b)
        step *= 2
    return items


def wrap(x, n):
    return x & (n - 1) if n & (n - 1) == 0 else lax.rem(x, n)


def cosines(turns, n):
    return jnp.cos(wrap(turns, n).astype(f32) * (2.0 * math.pi / n))


def modes_by_lane(modes, slots, count, lanes):
    width = count // len(slots)
    lane = lax.rem(lax.broadcasted_iota(jnp.int32, (8, lanes), 1), count)
    mode = jnp.zeros((8, lanes), jnp.int32)
    for i in range(count):
        mode = jnp.where(lane == i, modes[slots[i // width] * width + i % width], mode)
    return mode[:1]


def modes_by_row(modes, slots, count, lanes):
    width = count // len(slots)
    row = lax.broadcasted_iota(jnp.int32, (count, lanes), 0)
    mode = jnp.zeros((count, lanes), jnp.int32)
    for i in range(count):
        mode = jnp.where(row == i, modes[slots[i // width] * width + i % width], mode)
    return mode


def phi_slots(n_phi):
    return [slot ^ lax.axis_index("phi") for slot in range(n_phi)]


def gz_slots(n_gz):
    return [slot ^ lax.axis_index("gz") for slot in gz_order(n_gz)]


def build_tables(z_modes, phi_modes, phi_ref, z_ref, n_gz, n_phi):
    phi_local, lanes = phi_ref.shape[0] // 2, phi_ref.shape[1] // 2
    rows, z_local = z_ref.shape[0] // 2, z_ref.shape[1]
    kp, kz = lanes // 2, rows // 2
    n = n_phi * phi_local
    mode = modes_by_lane(phi_modes, phi_slots(n_phi), kp, lanes)
    lane = lax.broadcasted_iota(jnp.int32, (1, lanes), 1)
    quarter = jnp.where(lane < kp, 0, n // 4)
    position = lax.axis_index("phi") * phi_local + lax.broadcasted_iota(jnp.int32, (phi_local, lanes), 0)
    high, low = halves(cosines(position * mode + quarter, n))
    phi_ref[:phi_local, :lanes] = high
    phi_ref[:phi_local, lanes:] = low
    phi_ref[phi_local:, :lanes] = high
    phi_ref[phi_local:, lanes:] = jnp.zeros_like(low)

    n = n_gz * z_local
    mode = modes_by_row(z_modes, gz_slots(n_gz), kz, z_local)
    position = lax.axis_index("gz") * z_local + lax.broadcasted_iota(jnp.int32, (kz, z_local), 1)
    for part, quarter in enumerate((0, 3 * n // 4)):
        high, low = halves(cosines(position * mode + quarter, n))
        z_ref[part * kz : (part + 1) * kz] = high
        z_ref[rows + part * kz : rows + (part + 1) * kz] = low


def forward_kernel(
    z_modes, phi_modes, x_ref, t_ref, ak_ref, as_ref, bk_ref, bs_ref, phi_ref, z_ref, *, n_gz, n_phi
):
    at, count = pl.program_id(0), pl.num_programs(0)

    @pl.when(at == 0)
    def _():
        build_tables(z_modes, phi_modes, phi_ref, z_ref, n_gz, n_phi)

    width = phi_ref.shape[1] // (4 * n_phi)
    for first, keep_ref, send_ref in ((True, ak_ref, as_ref), (False, bk_ref, bs_ref)):

        @pl.when((at < count // 2) == first)
        def _():
            base = (at if first else at - count // 2) * x_ref.shape[0]
            transform(phi_ref, z_ref, x_ref, t_ref, keep_ref, send_ref, base, n_phi, width)


def transform(phi_ref, z_ref, x_ref, t_ref, keep_ref, send_ref, base, n_phi, width):
    block, cycles, z_local, phi_local = x_ref.shape
    modes2 = z_ref.shape[0] // 2
    modes = modes2 // 2
    lanes = phi_ref.shape[1] // 2
    shape = keep_ref.shape[1:-4] + keep_ref.shape[-2:]
    lane = lax.broadcasted_iota(jnp.int32, (modes, lanes), 1)
    sign = jnp.where(lane < lanes // 2, 1.0, -1.0).astype(f32)

    def along_phi(c, part):
        x = (x_ref, t_ref)[part][c].reshape(cycles * z_local, phi_local)
        high, low = halves(x)
        y = dot(jnp.concatenate([high, low], axis=1), phi_ref[...])
        high, low = halves(y[:, :lanes] + y[:, lanes:])
        return jnp.concatenate([high, low], axis=1)

    def along_z(y):
        return [dot(z_ref[...], y[r * z_local : (r + 1) * z_local]) for r in range(cycles)]

    def finish(c, products):
        items = []
        for m in products:
            m = m[:modes2, :lanes] + (m[:modes2, lanes:] + m[modes2:, :lanes])
            items.append(m[:modes] + sign * pltpu.roll(m[modes:], lanes // 2, 1))
        for group in range(len(items) // n_phi):
            part = exchange(items[group * n_phi : (group + 1) * n_phi], width)
            for slot, item in enumerate(part):
                out = keep_ref if slot % 2 == 0 else send_ref
                out[slot // 2, :, base + c, group, :, :] = item.reshape(shape)

    steps = [(c, part) for c in range(block) for part in range(2)]
    ahead = along_phi(*steps[0])
    products = []
    for i, (c, part) in enumerate(steps):
        y = ahead
        if i + 1 < len(steps):
            ahead = along_phi(*steps[i + 1])
        products.append(along_z(y))
        if part == 0 and c:
            finish(c - 1, products[-3] + products[-2])
    finish(block - 1, products[-2] + products[-1])


def forward(field, tangent, z_modes, phi_modes, n_phi, n_gz):
    channels, cycles, z_local, phi_local = field.shape
    groups = 2 * cycles // n_phi
    kz, kp = z_modes.shape[0], phi_modes.shape[0]
    lanes = 2 * kp
    out = pltpu.VMEM((n_phi // 2, n_gz, channels // 2, groups, kz // n_gz, lanes), f32)
    step = 4
    block = pl.BlockSpec((step, cycles, z_local, phi_local), lambda c: (c, 0, 0, 0))
    return pl.pallas_call(
        functools.partial(forward_kernel, n_gz=n_gz, n_phi=n_phi),
        grid=(channels // step,),
        in_specs=[pl.BlockSpec(memory_space=pltpu.SMEM)] * 2 + [block, block],
        out_specs=[pl.BlockSpec(memory_space=pltpu.VMEM)] * 4,
        out_shape=[out] * 4,
        scratch_shapes=[
            pltpu.VMEM((2 * phi_local, 2 * lanes), bf16),
            pltpu.VMEM((4 * kz, z_local), bf16),
        ],
        compiler_params=pltpu.CompilerParams(vmem_limit_bytes=40 * MIB),
        cost_estimate=pl.CostEstimate(
            flops=24 * field.size * lanes, bytes_accessed=8 * field.size, transcendentals=0
        ),
        name="forward_transform",
    )(z_modes, phi_modes, field, tangent)


def local_kernel(x_ref, t_ref, w_ref, bias_ref, xo_ref, to_ref):
    channels, _, rows, columns = x_ref.shape
    base = pl.multiple_of(pl.program_id(0) * rows, rows)
    tiles = [
        (ref, out, start) for ref, out in ((x_ref, xo_ref), (t_ref, to_ref)) for start in range(0, rows, 8)
    ]
    for at in range(0, len(tiles), 4):
        products = []
        for ref, _, start in tiles[at : at + 4]:
            high, low = halves(ref[:, 0, start : start + 8, :].reshape(channels * 8, columns))
            products.append(dot(w_ref[...], jnp.concatenate([high, low], axis=0)))
        for (_, out, start), m in zip(tiles[at : at + 4], products):
            m = (m[: channels * 8] + m[channels * 8 :]).reshape(channels, 8, columns)
            out[:, pl.ds(base + start, 8), :] = m + bias_ref[...] if out is xo_ref else m


def local_mix(field, tangent, weight, bias, cycle, part, parts):
    channels, _, z_local, phi_local = field.shape
    span = z_local // parts
    rows = min(64, span)
    steps = span // rows
    out = pltpu.VMEM((channels, span, phi_local), f32)
    block = pl.BlockSpec((channels, 1, rows, phi_local), lambda z: (0, cycle, part * steps + z, 0))
    out_block = pl.BlockSpec(memory_space=pltpu.VMEM)
    size = channels * span * phi_local
    return pl.pallas_call(
        local_kernel,
        grid=(steps,),
        in_specs=[
            block,
            block,
            pl.BlockSpec(weight.shape, lambda z: (0, 0)),
            pl.BlockSpec(bias.shape, lambda z: (0, 0, 0)),
        ],
        out_specs=[out_block, out_block],
        out_shape=[out, out],
        compiler_params=pltpu.CompilerParams(vmem_limit_bytes=16 * MIB),
        cost_estimate=pl.CostEstimate(flops=1024 * size, bytes_accessed=8 * size, transcendentals=0),
        name="local_mix",
    )(field, tangent, weight, bias)


def mix_kernel(s_ref, wr_ref, wi_ref, out_ref):
    channels = s_ref.shape[0]
    lanes = s_ref.shape[-1]
    total = jnp.zeros(out_ref.shape, f32)
    for c in range(channels):
        s = s_ref[c]
        turned = jnp.concatenate([s[..., lanes // 2 :], s[..., : lanes // 2]], axis=-1)
        total = total + s[None] * wr_ref[c][:, None] + turned[None] * wi_ref[c][:, None]
    out_ref[...] = total


def mix(spectrum, wr, wi):
    return pl.pallas_call(
        mix_kernel,
        out_shape=jax.ShapeDtypeStruct((wr.shape[1],) + spectrum.shape[1:], f32),
        compiler_params=pltpu.CompilerParams(vmem_limit_bytes=8 * MIB),
        name="mode_mix",
    )(spectrum, wr, wi)


def gelu_pair(x, t):
    a = math.sqrt(2.0 / math.pi)
    b = a * 0.044715
    square = x * x
    s = 0.5 + 0.5 * jnp.tanh(x * (a + b * square))
    out = x * s
    return out, t * (s + out * ((1.0 - s) * (2.0 * a + (6.0 * b) * square)))


def inverse_kernel(*refs, n_phi, width):
    own, other = refs[:4], refs[4:8]
    phi_ref, z_ref = refs[8:10]
    out_ref, out_t_ref = refs[-2:]
    refs = refs[10:-2]
    block, cycles, z_local, phi_local = out_ref.shape
    parts = len(refs) // (2 * cycles)
    span = z_local // parts
    groups, depth, lanes = own[0].shape[-3:]
    modes = z_ref.shape[1] // 6
    first = pl.program_id(0) < pl.num_programs(0) // 2
    at = pl.program_id(0) * block

    def slots(pieces, c, group):
        v, ab1, a2, b2 = pieces
        ab1 = ab1[:, c, group]
        low = [v[:, c, group], jnp.where(first, ab1, b2[0, :, c, group])]
        high = [
            jnp.where(first, a2[0, :, c, group], ab1),
            jnp.where(first, a2[1, :, c, group], b2[1, :, c, group]),
        ]
        return [jnp.concatenate(rows, axis=0).reshape(modes, lanes) for rows in (low, high)]

    for c in range(block):
        spectral = []
        for group in range(groups):
            pairs = zip(slots(own, c, group), slots(other, c, group))
            items = [item for pair in pairs for item in pair]
            high, low = halves(jnp.concatenate(exchange(items, width), axis=0))
            h = dot(jnp.concatenate([high, low, high], axis=1), phi_ref[...])
            for b in range(n_phi):
                part = h[b * modes : (b + 1) * modes]
                part = jnp.concatenate([part[:, :phi_local], part[:, phi_local:]], axis=0)
                high, low = halves(part)
                spectral.append(jnp.concatenate([high, high, low], axis=0))
        values = [dot(z_ref[...], part) for part in spectral]
        for r in range(cycles):
            for p in range(parts):
                rows = slice(p * span, (p + 1) * span)
                lx, lt = refs[2 * (r * parts + p) : 2 * (r * parts + p) + 2]
                x = values[r][rows] + lx[at + c]
                t = values[cycles + r][rows] + lt[at + c]
                out_ref[c, r, rows], out_t_ref[c, r, rows] = gelu_pair(x, t)


def inverse(own, other, phi_table, z_table, local, cycles, n_phi, width):
    channels, span, phi_local = local[0].shape
    z_local = span * len(local) // (2 * cycles)
    step = 2
    steps = channels // step
    zeros = lambda n: (0,) * n
    shape = (own[0].shape[0], step) + own[0].shape[2:]
    tail = zeros(len(shape) - 2)
    v_block = pl.BlockSpec(shape, lambda o: (0, o) + tail)
    a_block = pl.BlockSpec((2,) + shape, lambda o: (0, 0, jnp.minimum(o, steps // 2 - 1)) + tail)
    b_block = pl.BlockSpec((2,) + shape, lambda o: (0, 0, jnp.maximum(o - steps // 2, 0)) + tail)
    local_block = pl.BlockSpec(memory_space=pltpu.VMEM)
    local = [pltpu.with_memory_space_constraint(piece, pltpu.VMEM) for piece in local]
    out = jax.ShapeDtypeStruct((channels, cycles, z_local, phi_local), f32)
    out_block = pl.BlockSpec((step, cycles, z_local, phi_local), lambda o: (o, 0, 0, 0))
    size = channels * cycles * z_local * phi_local
    return pl.pallas_call(
        functools.partial(inverse_kernel, n_phi=n_phi, width=width),
        grid=(steps,),
        in_specs=[v_block, v_block, a_block, b_block] * 2
        + [
            pl.BlockSpec(phi_table.shape, lambda o: (0, 0)),
            pl.BlockSpec(z_table.shape, lambda o: (0, 0)),
        ]
        + [local_block] * len(local),
        out_specs=[out_block, out_block],
        out_shape=[out, out],
        compiler_params=pltpu.CompilerParams(vmem_limit_bytes=18 * MIB),
        cost_estimate=pl.CostEstimate(
            flops=1600 * size, bytes_accessed=16 * size, transcendentals=size
        ),
        name="inverse_transform",
    )(*own, *other, phi_table, z_table, *local)


def swap(x, axis, bit):
    count = lax.axis_size(axis)
    return lax.ppermute(x, axis, [(i, i ^ bit) for i in range(count)])


class Filler:
    def __init__(self, field, tangent, small, prepare, parts):
        self.inputs = (field, tangent)
        self.small = small
        self.prepare = prepare
        self.tables = None
        self.parts = parts
        self.todo = [(r, p) for r in range(field.shape[1]) for p in range(parts)]
        self.done = []

    def beside(self, sent, got, count=1):
        if self.tables is None:
            small, _ = lax.optimization_barrier((self.small, sent))
            self.tables = self.prepare(*small)
            got, self.tables = lax.optimization_barrier((got, self.tables))
            return got
        for _ in range(min(count, len(self.todo))):
            r, p = self.todo.pop(0)
            inputs, _ = lax.optimization_barrier((self.inputs, sent))
            piece = local_mix(*inputs, *self.tables[:2], r, p, self.parts)
            got, piece = lax.optimization_barrier((got, piece))
            self.done += piece
        return got


def sums_kernel(*refs, outputs):
    refs, outs = refs[: -len(outputs)], refs[-len(outputs) :]
    for out, parts in zip(outs, outputs):
        total = [functools.reduce(jnp.add, [refs[at][index] for at, index in part]) for part in parts]
        out[...] = total[0] if len(total) == 1 else jnp.concatenate(total, axis=1)


def sums(*outputs):
    arrays = []
    plan = []
    shapes = []
    for parts in outputs:
        entry = []
        for part in parts:
            terms = []
            for array, index in part:
                known = [i for i, other in enumerate(arrays) if other is array]
                if not known:
                    known = [len(arrays)]
                    arrays.append(array)
                terms.append((known[0], index))
            entry.append(terms)
        plan.append(entry)
        shape = list(jax.eval_shape(lambda x: x[parts[0][0][1]], parts[0][0][0]).shape)
        if len(parts) > 1:
            shape[1] *= len(parts)
        shapes.append(pltpu.VMEM(tuple(shape), f32))
    return pl.pallas_call(
        functools.partial(sums_kernel, outputs=plan),
        in_specs=[pl.BlockSpec(memory_space=pltpu.VMEM)] * len(arrays),
        out_specs=[pl.BlockSpec(memory_space=pltpu.VMEM)] * len(shapes),
        out_shape=shapes,
        compiler_params=pltpu.CompilerParams(vmem_limit_bytes=8 * MIB),
        name="add_terms",
    )(*[pltpu.with_memory_space_constraint(array, pltpu.VMEM) for array in arrays])


def reduce_scatter(a, b, n_phi, n_gz, filler):
    every, low, high = slice(None), slice(n_gz // 2), slice(n_gz // 2, None)
    a = [a[0], swap(a[1], "phi", 1)]
    b = [b[0], swap(b[1], "phi", 1)]
    (a_sent,) = sums([[(term, (1,)) for term in a]])
    (b_sent,) = sums([[(term, (every, high)) for term in b]])
    got = (swap(a_sent, "phi", 2), swap(b_sent, "gz", 1))
    a_got, b_got = filler.beside((a_sent, b_sent), got)
    a_sent, b_sent = sums(
        [[(term, (0, high)) for term in a] + [(a_got, (high,))]],
        [[(term, (1, low)) for term in b] + [(b_got, (1,))]],
    )
    got = (swap(a_sent, "gz", 1), swap(b_sent, "phi", 2))
    a_new, b_new = filler.beside((a_sent, b_sent), got)

    def rest(i, size):
        rows = slice(i * size, (i + 1) * size)
        return [
            [(term, (0, rows)) for term in a] + [(a_got, (rows,)), (a_new, (rows,))],
            [(term, (0, rows)) for term in b] + [(b_got, (0, rows)), (b_new, (rows,))],
        ]

    left = n_gz // 2
    for bits in gz_groups(n_gz):
        count = 1 << len(bits)
        size = left // count
        v, *sent = sums(*[rest(i, size) for i in range(count)])
        got = [swap(part, "gz", group_bits(i, bits)) for i, part in enumerate(sent, 1)]
        terms = [v, *filler.beside(sent, got, count // 2)]
        rest = lambda i, size: [[(term, (slice(i * size, (i + 1) * size),)) for term in terms]]
        left = size
    return functools.reduce(jnp.add, terms)[0]


def all_gather(v, n_phi, n_gz, filler):
    v = v[None]
    for bits in reversed(gz_groups(n_gz)):
        count = 1 << len(bits)
        got = [swap(v, "gz", group_bits(i, bits)) for i in range(1, count)]
        got = filler.beside(v, got, count // 2)
        v = jnp.concatenate([v, *got], axis=0)
    half = v.shape[1] // 2
    a, b = v[:, :half], v[:, half:]
    got = (swap(a, "gz", 1), swap(b, "phi", 2), swap(v, "phi", 1))
    a1, b1, v_core = filler.beside((a, b), got)
    ab1 = jnp.concatenate([a1, b1], axis=1)
    a, b = jnp.stack([a, a1]), jnp.stack([b, b1])
    got = (swap(a, "phi", 2), swap(b, "gz", 1), swap(ab1, "phi", 1))
    a2, b2, ab1_core = filler.beside((a, b), got, len(filler.todo))
    return (v, ab1, a2, b2), (v_core, ab1_core, swap(a2, "phi", 1), swap(b2, "phi", 1))


def gz_groups(n_gz):
    bits = list(range(1, n_gz.bit_length() - 1))
    return [bits[i : i + 2] for i in range(0, len(bits), 2)]


def group_bits(i, bits):
    digits = [(i >> (len(bits) - 1 - j)) & 1 for j in range(len(bits))]
    return sum(digit << bit for digit, bit in zip(digits, bits))


def gz_order(n_gz):
    bits = n_gz.bit_length() - 1
    return [
        sum(digit << i for i, digit in enumerate(digits))
        for digits in itertools.product((0, 1), repeat=bits)
    ]


def tables_kernel(
    z_modes, phi_modes, bias, weight_ref, modes_ref, local_ref, bias_ref, phi_ref, z_ref, wr_ref, wi_ref,
    *, n_gz, n_phi, scale
):
    channels = weight_ref.shape[0]
    rows = 8 * channels
    row = lax.broadcasted_iota(jnp.int32, (rows, channels), 0)
    copy = (row // 8 == lax.broadcasted_iota(jnp.int32, (rows, channels), 1)).astype(bf16)
    row = lax.broadcasted_iota(jnp.int32, (rows, rows), 0)
    column = lax.broadcasted_iota(jnp.int32, (rows, rows), 1)
    same = lax.rem(row, 8) == lax.rem(column, 8)
    last = (((1,), (1,)), ((), ()))
    for part, w in enumerate(halves(weight_ref[...])):
        wide = lax.dot_general(copy, w, last, preferred_element_type=f32).astype(bf16)
        wide = lax.dot_general(wide, copy, last, preferred_element_type=f32)
        wide = jnp.where(same, wide, 0.0).astype(bf16)
        local_ref[part * rows : (part + 1) * rows, :rows] = wide
        local_ref[part * rows : (part + 1) * rows, rows:] = wide
    for o in range(channels):
        bias_ref[o] = jnp.full(bias_ref.shape[1:], bias[o], f32)

    lanes = phi_ref.shape[0] // 3
    phi_local = phi_ref.shape[1] // 2
    kp = lanes // 2
    n = n_phi * phi_local
    mode = modes_by_row(phi_modes, phi_slots(n_phi), kp, phi_local)
    position = lax.axis_index("phi") * phi_local + lax.broadcasted_iota(jnp.int32, (kp, phi_local), 1)
    turns = position * mode
    cosine = halves(cosines(turns, n))
    sine = halves(cosines(turns + 3 * n // 4, n))
    minus = halves(cosines(turns + n // 4, n))
    for i, part in enumerate((0, 0, 1)):
        at = i * lanes
        phi_ref[at : at + kp, :phi_local] = cosine[part]
        phi_ref[at : at + kp, phi_local:] = sine[part]
        phi_ref[at + kp : at + lanes, :phi_local] = minus[part]
        phi_ref[at + kp : at + lanes, phi_local:] = cosine[part]

    z_local, both = z_ref.shape[0], z_ref.shape[1] // 3
    kz = both // 2
    n = n_gz * z_local
    mode = modes_by_lane(z_modes, gz_slots(n_gz), kz, both)
    quarter = jnp.where(lax.broadcasted_iota(jnp.int32, (1, both), 1) < kz, 0, n // 4)
    position = lax.axis_index("gz") * z_local + lax.broadcasted_iota(jnp.int32, (z_local, both), 0)
    high, low = halves(cosines(position * mode + quarter, n))
    for i, part in enumerate((high, low, high)):
        z_ref[:, i * both : (i + 1) * both] = part

    width = kp // n_phi
    lane = lax.broadcasted_iota(jnp.int32, (width, lanes), 1)
    copy = (lax.rem(lane, width) == lax.broadcasted_iota(jnp.int32, (width, lanes), 0)).astype(bf16)
    sign = jnp.where(lax.broadcasted_iota(jnp.int32, (1, lanes), 1) < kp, -scale, scale).astype(f32)
    for part, (out, factor) in enumerate(((wr_ref, scale), (wi_ref, sign))):
        left = modes_ref[part]
        total = jnp.zeros(out.shape, f32)
        for _ in range(3):
            term = left.astype(bf16)
            left = left - term.astype(f32)
            total = total + dot(term, copy)
        out[...] = total * factor


def tables(spectral_weight, local_weight, bias_term, z_modes, phi_modes, z_local, phi_local):
    n_gz = lax.axis_size("gz")
    n_phi = lax.axis_size("phi")
    kz, kp = z_modes.shape[0], phi_modes.shape[0]
    channels = local_weight.shape[0]
    depth, width = spectral_weight.shape[-2:]
    rows = channels * channels * depth
    scale = (1.0 / math.sqrt(z_local * n_gz * phi_local * n_phi)) * (2.0 / math.sqrt(kz * kp))
    vmem, smem = pl.BlockSpec(memory_space=pltpu.VMEM), pl.BlockSpec(memory_space=pltpu.SMEM)
    *result, wr, wi = pl.pallas_call(
        functools.partial(tables_kernel, n_gz=n_gz, n_phi=n_phi, scale=scale),
        in_specs=[smem, smem, smem, vmem, vmem],
        out_specs=[vmem] * 6,
        out_shape=[
            jax.ShapeDtypeStruct((16 * channels, 16 * channels), bf16),
            jax.ShapeDtypeStruct((channels, 8, phi_local), f32),
            jax.ShapeDtypeStruct((6 * kp, 2 * phi_local), bf16),
            jax.ShapeDtypeStruct((z_local, 6 * kz), bf16),
            jax.ShapeDtypeStruct((rows, 2 * kp), f32),
            jax.ShapeDtypeStruct((rows, 2 * kp), f32),
        ],
        compiler_params=pltpu.CompilerParams(vmem_limit_bytes=16 * MIB),
        name="small_tables",
    )(z_modes, phi_modes, bias_term, local_weight, spectral_weight.reshape(2, rows, width))
    shape = (channels, channels, depth, 2 * kp)
    return *result, wr.reshape(shape), wi.reshape(shape)


def body(field, field_tangent, spectral_weight, local_weight, bias_term, z_modes, phi_modes):
    channels, cycles, z_local, phi_local = field.shape
    n_gz = lax.axis_size("gz")
    n_phi = lax.axis_size("phi")
    width = phi_modes.shape[0] // n_phi
    small = (spectral_weight, local_weight, bias_term, z_modes, phi_modes)
    prepare = functools.partial(tables, z_local=z_local, phi_local=phi_local)
    field = pltpu.with_memory_space_constraint(field, pltpu.HBM)
    field_tangent = pltpu.with_memory_space_constraint(field_tangent, pltpu.HBM)
    filler = Filler(field, field_tangent, small, prepare, 2)

    ak, asent, bk, bsent = forward(field, field_tangent, z_modes, phi_modes, n_phi, n_gz)
    spectrum = reduce_scatter((ak, asent), (bk, bsent), n_phi, n_gz, filler)
    _, _, phi_back, z_back, wr, wi = filler.tables
    mixed = mix(spectrum, wr, wi)
    own, other = all_gather(mixed, n_phi, n_gz, filler)
    return inverse(own, other, phi_back, z_back, filler.done, cycles, n_phi, width)


def solution(mesh):
    return jax.shard_map(
        body,
        mesh=mesh,
        in_specs=(
            P(None, None, "gz", "phi"),
            P(None, None, "gz", "phi"),
            P(None, None, None, "gz", "phi"),
            P(),
            P(),
            P(),
            P(),
        ),
        out_specs=(P(None, None, "gz", "phi"), P(None, None, "gz", "phi")),
        check_vma=False,
    )
```

```python
import functools
import itertools
import math

import jax
import jax.numpy as jnp
from jax import lax
from jax.experimental import pallas as pl
from jax.experimental.pallas import tpu as pltpu
from jax.sharding import PartitionSpec as P

f32 = jnp.float32
bf16 = jnp.bfloat16
MIB = 1024 * 1024


def halves(x):
    high = x.astype(bf16)
    return high, (x - high.astype(f32)).astype(bf16)


def dot(a, b):
    return lax.dot_general(a, b, (((1,), (0,)), ((), ())), preferred_element_type=f32)


def exchange(items, width):
    items = list(items)
    count = len(items)
    lanes = items[0].shape[-1]
    lane = lax.broadcasted_iota(jnp.int32, items[0].shape, items[0].ndim - 1)
    step = 1
    while step < count:
        shift = width * step
        low = (lane // shift) % 2 == 0
        for i in range(count):
            if i & step:
                continue
            a, b = items[i], items[i | step]
            items[i] = jnp.where(low, a, pltpu.roll(b, shift, 1))
            items[i | step] = jnp.where(low, pltpu.roll(a, lanes - shift, 1), b)
        step *= 2
    return items


def wrap(x, n):
    return x & (n - 1) if n & (n - 1) == 0 else lax.rem(x, n)


def cosines(turns, n):
    return jnp.cos(wrap(turns, n).astype(f32) * (2.0 * math.pi / n))


def modes_by_lane(modes, slots, count, lanes):
    width = count // len(slots)
    lane = lax.rem(lax.broadcasted_iota(jnp.int32, (8, lanes), 1), count)
    mode = jnp.zeros((8, lanes), jnp.int32)
    for i in range(count):
        mode = jnp.where(lane == i, modes[slots[i // width] * width + i % width], mode)
    return mode[:1]


def modes_by_row(modes, slots, count, lanes):
    width = count // len(slots)
    row = lax.broadcasted_iota(jnp.int32, (count, lanes), 0)
    mode = jnp.zeros((count, lanes), jnp.int32)
    for i in range(count):
        mode = jnp.where(row == i, modes[slots[i // width] * width + i % width], mode)
    return mode


def phi_slots(n_phi):
    return [slot ^ lax.axis_index("phi") for slot in range(n_phi)]


def gz_slots(n_gz):
    return [slot ^ lax.axis_index("gz") for slot in gz_order(n_gz)]


def build_tables(z_modes, phi_modes, phi_ref, z_ref, n_gz, n_phi):
    phi_local, lanes = phi_ref.shape[0] // 2, phi_ref.shape[1] // 2
    z_local = z_ref.shape[1] // 3
    kp, kz = lanes // 2, z_ref.shape[0] // 2
    n = n_phi * phi_local
    mode = modes_by_lane(phi_modes, phi_slots(n_phi), kp, lanes)
    lane = lax.broadcasted_iota(jnp.int32, (1, lanes), 1)
    quarter = jnp.where(lane < kp, 0, n // 4)
    position = lax.axis_index("phi") * phi_local + lax.broadcasted_iota(jnp.int32, (phi_local, lanes), 0)
    high, low = halves(cosines(position * mode + quarter, n))
    phi_ref[:phi_local, :lanes] = high
    phi_ref[:phi_local, lanes:] = low
    phi_ref[phi_local:, :lanes] = high
    phi_ref[phi_local:, lanes:] = jnp.zeros_like(low)

    n = n_gz * z_local
    mode = modes_by_row(z_modes, gz_slots(n_gz), kz, z_local)
    position = lax.axis_index("gz") * z_local + lax.broadcasted_iota(jnp.int32, (kz, z_local), 1)
    for part, quarter in enumerate((0, 3 * n // 4)):
        high, low = halves(cosines(position * mode + quarter, n))
        for i, term in enumerate((high, low, high)):
            z_ref[part * kz : (part + 1) * kz, i * z_local : (i + 1) * z_local] = term


def forward_kernel(
    z_modes, phi_modes, x_ref, t_ref, ak_ref, as_ref, bk_ref, bs_ref, phi_ref, z_ref, *, n_gz, n_phi
):
    at, count = pl.program_id(0), pl.num_programs(0)

    @pl.when(at == 0)
    def _():
        build_tables(z_modes, phi_modes, phi_ref, z_ref, n_gz, n_phi)

    width = phi_ref.shape[1] // (4 * n_phi)
    for first, keep_ref, send_ref in ((True, ak_ref, as_ref), (False, bk_ref, bs_ref)):

        @pl.when((at < count // 2) == first)
        def _():
            base = (at if first else at - count // 2) * x_ref.shape[0]
            transform(phi_ref, z_ref, x_ref, t_ref, keep_ref, send_ref, base, n_phi, width)


def transform(phi_ref, z_ref, x_ref, t_ref, keep_ref, send_ref, base, n_phi, width):
    block, cycles, z_local, phi_local = x_ref.shape
    modes = z_ref.shape[0] // 2
    lanes = phi_ref.shape[1] // 2
    shape = keep_ref.shape[1:-4] + keep_ref.shape[-2:]
    lane = lax.broadcasted_iota(jnp.int32, (modes, lanes), 1)
    sign = jnp.where(lane < lanes // 2, 1.0, -1.0).astype(f32)

    def along_phi(c, part):
        x = (x_ref, t_ref)[part][c].reshape(cycles * z_local, phi_local)
        high, low = halves(x)
        y = dot(jnp.concatenate([high, low], axis=1), phi_ref[...])
        high, low = (
            jnp.concatenate([term[r * z_local : (r + 1) * z_local] for r in range(cycles)], axis=1)
            for term in halves(y[:, :lanes] + y[:, lanes:])
        )
        return jnp.concatenate([high, high, low], axis=0)

    def along_z(y):
        m = dot(z_ref[...], y)
        return [m[:, r * lanes : (r + 1) * lanes] for r in range(cycles)]

    def finish(c, products):
        items = []
        for m in products:
            items.append(m[:modes] + sign * pltpu.roll(m[modes:], lanes // 2, 1))
        for group in range(len(items) // n_phi):
            part = exchange(items[group * n_phi : (group + 1) * n_phi], width)
            for slot, item in enumerate(part):
                out = keep_ref if slot % 2 == 0 else send_ref
                out[slot // 2, :, base + c, group, :, :] = item.reshape(shape)

    steps = [(c, part) for c in range(block) for part in range(2)]
    ahead = along_phi(*steps[0])
    products = []
    for i, (c, part) in enumerate(steps):
        y = ahead
        if i + 1 < len(steps):
            ahead = along_phi(*steps[i + 1])
        products.append(along_z(y))
        if part == 0 and c:
            finish(c - 1, products[-3] + products[-2])
    finish(block - 1, products[-2] + products[-1])


def forward(field, tangent, z_modes, phi_modes, n_phi, n_gz):
    channels, cycles, z_local, phi_local = field.shape
    groups = 2 * cycles // n_phi
    kz, kp = z_modes.shape[0], phi_modes.shape[0]
    lanes = 2 * kp
    out = pltpu.VMEM((n_phi // 2, n_gz, channels // 2, groups, kz // n_gz, lanes), f32)
    step = 4
    block = pl.BlockSpec((step, cycles, z_local, phi_local), lambda c: (c, 0, 0, 0))
    return pl.pallas_call(
        functools.partial(forward_kernel, n_gz=n_gz, n_phi=n_phi),
        grid=(channels // step,),
        in_specs=[pl.BlockSpec(memory_space=pltpu.SMEM)] * 2 + [block, block],
        out_specs=[pl.BlockSpec(memory_space=pltpu.VMEM)] * 4,
        out_shape=[out] * 4,
        scratch_shapes=[
            pltpu.VMEM((2 * phi_local, 2 * lanes), bf16),
            pltpu.VMEM((2 * kz, 3 * z_local), bf16),
        ],
        compiler_params=pltpu.CompilerParams(vmem_limit_bytes=54 * MIB),
        cost_estimate=pl.CostEstimate(
            flops=24 * field.size * lanes, bytes_accessed=8 * field.size, transcendentals=0
        ),
        name="forward_transform",
    )(z_modes, phi_modes, field, tangent)


def local_kernel(x_ref, t_ref, w_ref, bias_ref, xo_ref, to_ref):
    channels, _, rows, columns = x_ref.shape
    base = pl.multiple_of(pl.program_id(0) * rows, rows)
    tiles = [
        (ref, out, start) for ref, out in ((x_ref, xo_ref), (t_ref, to_ref)) for start in range(0, rows, 8)
    ]
    for at in range(0, len(tiles), 4):
        products = []
        for ref, _, start in tiles[at : at + 4]:
            high, low = halves(ref[:, 0, start : start + 8, :].reshape(channels * 8, columns))
            products.append(dot(w_ref[...], jnp.concatenate([high, low], axis=0)))
        for (_, out, start), m in zip(tiles[at : at + 4], products):
            m = (m[: channels * 8] + m[channels * 8 :]).reshape(channels, 8, columns)
            out[:, pl.ds(base + start, 8), :] = m + bias_ref[...] if out is xo_ref else m


def local_mix(field, tangent, weight, bias, cycle, part, parts):
    channels, _, z_local, phi_local = field.shape
    span = z_local // parts
    rows = min(64, span)
    steps = span // rows
    out = pltpu.VMEM((channels, span, phi_local), f32)
    block = pl.BlockSpec((channels, 1, rows, phi_local), lambda z: (0, cycle, part * steps + z, 0))
    out_block = pl.BlockSpec(memory_space=pltpu.VMEM)
    size = channels * span * phi_local
    return pl.pallas_call(
        local_kernel,
        grid=(steps,),
        in_specs=[
            block,
            block,
            pl.BlockSpec(weight.shape, lambda z: (0, 0)),
            pl.BlockSpec(bias.shape, lambda z: (0, 0, 0)),
        ],
        out_specs=[out_block, out_block],
        out_shape=[out, out],
        compiler_params=pltpu.CompilerParams(vmem_limit_bytes=16 * MIB),
        cost_estimate=pl.CostEstimate(flops=1024 * size, bytes_accessed=8 * size, transcendentals=0),
        name="local_mix",
    )(field, tangent, weight, bias)


def mix_kernel(s_ref, wr_ref, wi_ref, out_ref):
    channels = s_ref.shape[0]
    lanes = s_ref.shape[-1]
    total = jnp.zeros(out_ref.shape, f32)
    for c in range(channels):
        s = s_ref[c]
        turned = jnp.concatenate([s[..., lanes // 2 :], s[..., : lanes // 2]], axis=-1)
        total = total + s[None] * wr_ref[c][:, None] + turned[None] * wi_ref[c][:, None]
    out_ref[...] = total


def mix(spectrum, wr, wi):
    return pl.pallas_call(
        mix_kernel,
        out_shape=jax.ShapeDtypeStruct((wr.shape[1],) + spectrum.shape[1:], f32),
        compiler_params=pltpu.CompilerParams(vmem_limit_bytes=8 * MIB),
        name="mode_mix",
    )(spectrum, wr, wi)


def gelu_pair(x, t):
    a = math.sqrt(2.0 / math.pi)
    b = a * 0.044715
    square = x * x
    s = 0.5 + 0.5 * jnp.tanh(x * (a + b * square))
    out = x * s
    return out, t * (s + out * ((1.0 - s) * (2.0 * a + (6.0 * b) * square)))


def inverse_kernel(*refs, n_phi, width):
    own, other = refs[:4], refs[4:8]
    phi_ref, z_ref = refs[8:10]
    out_ref, out_t_ref = refs[-2:]
    refs = refs[10:-2]
    block, cycles, z_local, phi_local = out_ref.shape
    parts = len(refs) // (2 * cycles)
    span = z_local // parts
    groups, depth, lanes = own[0].shape[-3:]
    modes = z_ref.shape[1] // 6
    first = pl.program_id(0) < pl.num_programs(0) // 2
    at = pl.program_id(0) * block

    def slots(pieces, c, group):
        v, ab1, a2, b2 = pieces
        half = a2.shape[2]
        a_at, b_at = jnp.minimum(at + c, half - 1), jnp.maximum(at + c - half, 0)
        ab1 = ab1[:, at + c, group]
        low = [v[:, at + c, group], jnp.where(first, ab1, b2[0, :, b_at, group])]
        high = [
            jnp.where(first, a2[0, :, a_at, group], ab1),
            jnp.where(first, a2[1, :, a_at, group], b2[1, :, b_at, group]),
        ]
        return [jnp.concatenate(rows, axis=0).reshape(modes, lanes) for rows in (low, high)]

    for c in range(block):
        spectral = []
        for group in range(groups):
            pairs = zip(slots(own, c, group), slots(other, c, group))
            items = [item for pair in pairs for item in pair]
            high, low = halves(jnp.concatenate(exchange(items, width), axis=0))
            h = dot(jnp.concatenate([high, low, high], axis=1), phi_ref[...])
            for b in range(n_phi):
                part = h[b * modes : (b + 1) * modes]
                part = jnp.concatenate([part[:, :phi_local], part[:, phi_local:]], axis=0)
                high, low = halves(part)
                spectral.append(jnp.concatenate([high, high, low], axis=0))
        values = [dot(z_ref[...], part) for part in spectral]
        for r in range(cycles):
            for p in range(parts):
                rows = slice(p * span, (p + 1) * span)
                lx, lt = refs[2 * (r * parts + p) : 2 * (r * parts + p) + 2]
                x = values[r][rows] + lx[at + c]
                t = values[cycles + r][rows] + lt[at + c]
                out_ref[c, r, rows], out_t_ref[c, r, rows] = gelu_pair(x, t)


def inverse(own, other, phi_table, z_table, local, cycles, n_phi, width):
    channels, span, phi_local = local[0].shape
    z_local = span * len(local) // (2 * cycles)
    step = 2
    steps = channels // step
    held = pl.BlockSpec(memory_space=pltpu.VMEM)
    own, other, local = (
        [pltpu.with_memory_space_constraint(piece, pltpu.VMEM) for piece in pieces]
        for pieces in (own, other, local)
    )
    out = jax.ShapeDtypeStruct((channels, cycles, z_local, phi_local), f32)
    out_block = pl.BlockSpec((step, cycles, z_local, phi_local), lambda o: (o, 0, 0, 0))
    size = channels * cycles * z_local * phi_local
    return pl.pallas_call(
        functools.partial(inverse_kernel, n_phi=n_phi, width=width),
        grid=(steps,),
        in_specs=[held] * 8
        + [
            pl.BlockSpec(phi_table.shape, lambda o: (0, 0)),
            pl.BlockSpec(z_table.shape, lambda o: (0, 0)),
        ]
        + [held] * len(local),
        out_specs=[out_block, out_block],
        out_shape=[out, out],
        compiler_params=pltpu.CompilerParams(vmem_limit_bytes=18 * MIB),
        cost_estimate=pl.CostEstimate(
            flops=1600 * size, bytes_accessed=16 * size, transcendentals=size
        ),
        name="inverse_transform",
    )(*own, *other, phi_table, z_table, *local)


def swap(x, axis, bit):
    count = lax.axis_size(axis)
    return lax.ppermute(x, axis, [(i, i ^ bit) for i in range(count)])


class Filler:
    def __init__(self, field, tangent, small, prepare, parts):
        self.inputs = (field, tangent)
        self.small = small
        self.prepare = prepare
        self.tables = None
        self.parts = parts
        self.todo = [(r, p) for r in range(field.shape[1]) for p in range(parts)]
        self.done = []

    def beside(self, sent, got, count=1):
        if self.tables is None:
            small, _ = lax.optimization_barrier((self.small, sent))
            self.tables = self.prepare(*small)
            got, self.tables = lax.optimization_barrier((got, self.tables))
            return got
        for _ in range(min(count, len(self.todo))):
            r, p = self.todo.pop(0)
            inputs, _ = lax.optimization_barrier((self.inputs, sent))
            piece = local_mix(*inputs, *self.tables[:2], r, p, self.parts)
            got, piece = lax.optimization_barrier((got, piece))
            self.done += piece
        return got


def sums_kernel(*refs, outputs):
    refs, outs = refs[: -len(outputs)], refs[-len(outputs) :]
    for out, parts in zip(outs, outputs):
        total = [functools.reduce(jnp.add, [refs[at][index] for at, index in part]) for part in parts]
        out[...] = total[0] if len(total) == 1 else jnp.concatenate(total, axis=1)


def sums(*outputs):
    arrays = []
    plan = []
    shapes = []
    for parts in outputs:
        entry = []
        for part in parts:
            terms = []
            for array, index in part:
                known = [i for i, other in enumerate(arrays) if other is array]
                if not known:
                    known = [len(arrays)]
                    arrays.append(array)
                terms.append((known[0], index))
            entry.append(terms)
        plan.append(entry)
        shape = list(jax.eval_shape(lambda x: x[parts[0][0][1]], parts[0][0][0]).shape)
        if len(parts) > 1:
            shape[1] *= len(parts)
        shapes.append(pltpu.VMEM(tuple(shape), f32))
    return pl.pallas_call(
        functools.partial(sums_kernel, outputs=plan),
        in_specs=[pl.BlockSpec(memory_space=pltpu.VMEM)] * len(arrays),
        out_specs=[pl.BlockSpec(memory_space=pltpu.VMEM)] * len(shapes),
        out_shape=shapes,
        compiler_params=pltpu.CompilerParams(vmem_limit_bytes=8 * MIB),
        name="add_terms",
    )(*[pltpu.with_memory_space_constraint(array, pltpu.VMEM) for array in arrays])


def reduce_scatter(a, b, n_phi, n_gz, filler):
    every, low, high = slice(None), slice(n_gz // 2), slice(n_gz // 2, None)
    a = [a[0], swap(a[1], "phi", 1)]
    b = [b[0], swap(b[1], "phi", 1)]
    (a_sent,) = sums([[(term, (1,)) for term in a]])
    (b_sent,) = sums([[(term, (every, high)) for term in b]])
    got = (swap(a_sent, "phi", 2), swap(b_sent, "gz", 1))
    a_got, b_got = filler.beside((a_sent, b_sent), got)
    a_sent, b_sent = sums(
        [[(term, (0, high)) for term in a] + [(a_got, (high,))]],
        [[(term, (1, low)) for term in b] + [(b_got, (1,))]],
    )
    got = (swap(a_sent, "gz", 1), swap(b_sent, "phi", 2))
    a_new, b_new = filler.beside((a_sent, b_sent), got)

    def rest(i, size):
        rows = slice(i * size, (i + 1) * size)
        return [
            [(term, (0, rows)) for term in a] + [(a_got, (rows,)), (a_new, (rows,))],
            [(term, (0, rows)) for term in b] + [(b_got, (0, rows)), (b_new, (rows,))],
        ]

    left = n_gz // 2
    for bits in gz_groups(n_gz):
        count = 1 << len(bits)
        size = left // count
        v, *sent = sums(*[rest(i, size) for i in range(count)])
        got = [swap(part, "gz", group_bits(i, bits)) for i, part in enumerate(sent, 1)]
        terms = [v, *filler.beside(sent, got, count // 2)]
        rest = lambda i, size: [[(term, (slice(i * size, (i + 1) * size),)) for term in terms]]
        left = size
    return functools.reduce(jnp.add, terms)[0]


def all_gather(v, n_phi, n_gz, filler):
    v = v[None]
    for bits in reversed(gz_groups(n_gz)):
        count = 1 << len(bits)
        got = [swap(v, "gz", group_bits(i, bits)) for i in range(1, count)]
        got = filler.beside(v, got, count // 2)
        v = jnp.concatenate([v, *got], axis=0)
    half = v.shape[1] // 2
    a, b = v[:, :half], v[:, half:]
    got = (swap(a, "gz", 1), swap(b, "phi", 2), swap(v, "phi", 1))
    a1, b1, v_core = filler.beside((a, b), got)
    ab1 = jnp.concatenate([a1, b1], axis=1)
    a, b = jnp.stack([a, a1]), jnp.stack([b, b1])
    got = (swap(a, "phi", 2), swap(b, "gz", 1), swap(ab1, "phi", 1))
    a2, b2, ab1_core = filler.beside((a, b), got, len(filler.todo))
    return (v, ab1, a2, b2), (v_core, ab1_core, swap(a2, "phi", 1), swap(b2, "phi", 1))


def gz_groups(n_gz):
    bits = list(range(1, n_gz.bit_length() - 1))
    return [bits[i : i + 2] for i in range(0, len(bits), 2)]


def group_bits(i, bits):
    digits = [(i >> (len(bits) - 1 - j)) & 1 for j in range(len(bits))]
    return sum(digit << bit for digit, bit in zip(digits, bits))


def gz_order(n_gz):
    bits = n_gz.bit_length() - 1
    return [
        sum(digit << i for i, digit in enumerate(digits))
        for digits in itertools.product((0, 1), repeat=bits)
    ]


def tables_kernel(
    z_modes, phi_modes, bias, weight_ref, modes_ref, local_ref, bias_ref, phi_ref, z_ref, wr_ref, wi_ref,
    *, n_gz, n_phi, scale
):
    channels = weight_ref.shape[0]
    rows = 8 * channels
    row = lax.broadcasted_iota(jnp.int32, (rows, channels), 0)
    copy = (row // 8 == lax.broadcasted_iota(jnp.int32, (rows, channels), 1)).astype(bf16)
    row = lax.broadcasted_iota(jnp.int32, (rows, rows), 0)
    column = lax.broadcasted_iota(jnp.int32, (rows, rows), 1)
    same = lax.rem(row, 8) == lax.rem(column, 8)
    last = (((1,), (1,)), ((), ()))
    for part, w in enumerate(halves(weight_ref[...])):
        wide = lax.dot_general(copy, w, last, preferred_element_type=f32).astype(bf16)
        wide = lax.dot_general(wide, copy, last, preferred_element_type=f32)
        wide = jnp.where(same, wide, 0.0).astype(bf16)
        local_ref[part * rows : (part + 1) * rows, :rows] = wide
        local_ref[part * rows : (part + 1) * rows, rows:] = wide
    for o in range(channels):
        bias_ref[o] = jnp.full(bias_ref.shape[1:], bias[o], f32)

    lanes = phi_ref.shape[0] // 3
    phi_local = phi_ref.shape[1] // 2
    kp = lanes // 2
    n = n_phi * phi_local
    mode = modes_by_row(phi_modes, phi_slots(n_phi), kp, phi_local)
    position = lax.axis_index("phi") * phi_local + lax.broadcasted_iota(jnp.int32, (kp, phi_local), 1)
    turns = position * mode
    cosine = halves(cosines(turns, n))
    sine = halves(cosines(turns + 3 * n // 4, n))
    minus = halves(cosines(turns + n // 4, n))
    for i, part in enumerate((0, 0, 1)):
        at = i * lanes
        phi_ref[at : at + kp, :phi_local] = cosine[part]
        phi_ref[at : at + kp, phi_local:] = sine[part]
        phi_ref[at + kp : at + lanes, :phi_local] = minus[part]
        phi_ref[at + kp : at + lanes, phi_local:] = cosine[part]

    z_local, both = z_ref.shape[0], z_ref.shape[1] // 3
    kz = both // 2
    n = n_gz * z_local
    mode = modes_by_lane(z_modes, gz_slots(n_gz), kz, both)
    quarter = jnp.where(lax.broadcasted_iota(jnp.int32, (1, both), 1) < kz, 0, n // 4)
    position = lax.axis_index("gz") * z_local + lax.broadcasted_iota(jnp.int32, (z_local, both), 0)
    high, low = halves(cosines(position * mode + quarter, n))
    for i, part in enumerate((high, low, high)):
        z_ref[:, i * both : (i + 1) * both] = part

    width = kp // n_phi
    lane = lax.broadcasted_iota(jnp.int32, (width, lanes), 1)
    copy = (lax.rem(lane, width) == lax.broadcasted_iota(jnp.int32, (width, lanes), 0)).astype(bf16)
    sign = jnp.where(lax.broadcasted_iota(jnp.int32, (1, lanes), 1) < kp, -scale, scale).astype(f32)
    for part, (out, factor) in enumerate(((wr_ref, scale), (wi_ref, sign))):
        left = modes_ref[part]
        total = jnp.zeros(out.shape, f32)
        for _ in range(3):
            term = left.astype(bf16)
            left = left - term.astype(f32)
            total = total + dot(term, copy)
        out[...] = total * factor


def tables(spectral_weight, local_weight, bias_term, z_modes, phi_modes, z_local, phi_local):
    n_gz = lax.axis_size("gz")
    n_phi = lax.axis_size("phi")
    kz, kp = z_modes.shape[0], phi_modes.shape[0]
    channels = local_weight.shape[0]
    depth, width = spectral_weight.shape[-2:]
    rows = channels * channels * depth
    scale = (1.0 / math.sqrt(z_local * n_gz * phi_local * n_phi)) * (2.0 / math.sqrt(kz * kp))
    vmem, smem = pl.BlockSpec(memory_space=pltpu.VMEM), pl.BlockSpec(memory_space=pltpu.SMEM)
    *result, wr, wi = pl.pallas_call(
        functools.partial(tables_kernel, n_gz=n_gz, n_phi=n_phi, scale=scale),
        in_specs=[smem, smem, smem, vmem, vmem],
        out_specs=[vmem] * 6,
        out_shape=[
            jax.ShapeDtypeStruct((16 * channels, 16 * channels), bf16),
            jax.ShapeDtypeStruct((channels, 8, phi_local), f32),
            jax.ShapeDtypeStruct((6 * kp, 2 * phi_local), bf16),
            jax.ShapeDtypeStruct((z_local, 6 * kz), bf16),
            jax.ShapeDtypeStruct((rows, 2 * kp), f32),
            jax.ShapeDtypeStruct((rows, 2 * kp), f32),
        ],
        compiler_params=pltpu.CompilerParams(vmem_limit_bytes=16 * MIB),
        name="small_tables",
    )(z_modes, phi_modes, bias_term, local_weight, spectral_weight.reshape(2, rows, width))
    shape = (channels, channels, depth, 2 * kp)
    return *result, wr.reshape(shape), wi.reshape(shape)


def body(field, field_tangent, spectral_weight, local_weight, bias_term, z_modes, phi_modes):
    channels, cycles, z_local, phi_local = field.shape
    n_gz = lax.axis_size("gz")
    n_phi = lax.axis_size("phi")
    width = phi_modes.shape[0] // n_phi
    small = (spectral_weight, local_weight, bias_term, z_modes, phi_modes)
    prepare = functools.partial(tables, z_local=z_local, phi_local=phi_local)
    field = pltpu.with_memory_space_constraint(field, pltpu.HBM)
    field_tangent = pltpu.with_memory_space_constraint(field_tangent, pltpu.HBM)
    filler = Filler(field, field_tangent, small, prepare, 2)

    ak, asent, bk, bsent = forward(field, field_tangent, z_modes, phi_modes, n_phi, n_gz)
    spectrum = reduce_scatter((ak, asent), (bk, bsent), n_phi, n_gz, filler)
    _, _, phi_back, z_back, wr, wi = filler.tables
    mixed = mix(spectrum, wr, wi)
    own, other = all_gather(mixed, n_phi, n_gz, filler)
    return inverse(own, other, phi_back, z_back, filler.done, cycles, n_phi, width)


def solution(mesh):
    return jax.shard_map(
        body,
        mesh=mesh,
        in_specs=(
            P(None, None, "gz", "phi"),
            P(None, None, "gz", "phi"),
            P(None, None, None, "gz", "phi"),
            P(),
            P(),
            P(),
            P(),
        ),
        out_specs=(P(None, None, "gz", "phi"), P(None, None, "gz", "phi")),
        check_vma=False,
    )
```

```python
import functools
import itertools
import math

import jax
import jax.numpy as jnp
from jax import lax
from jax.experimental import pallas as pl
from jax.experimental.pallas import tpu as pltpu
from jax.sharding import PartitionSpec as P

f32 = jnp.float32
bf16 = jnp.bfloat16
MIB = 1024 * 1024


def halves(x):
    high = x.astype(bf16)
    return high, (x - high.astype(f32)).astype(bf16)


def dot(a, b):
    return lax.dot_general(a, b, (((1,), (0,)), ((), ())), preferred_element_type=f32)


def exchange(items, width):
    items = list(items)
    count = len(items)
    lanes = items[0].shape[-1]
    lane = lax.broadcasted_iota(jnp.int32, items[0].shape, items[0].ndim - 1)
    step = 1
    while step < count:
        shift = width * step
        low = (lane // shift) % 2 == 0
        for i in range(count):
            if i & step:
                continue
            a, b = items[i], items[i | step]
            items[i] = jnp.where(low, a, pltpu.roll(b, shift, 1))
            items[i | step] = jnp.where(low, pltpu.roll(a, lanes - shift, 1), b)
        step *= 2
    return items


def wrap(x, n):
    return x & (n - 1) if n & (n - 1) == 0 else lax.rem(x, n)


def cosines(turns, n):
    return jnp.cos(wrap(turns, n).astype(f32) * (2.0 * math.pi / n))


def modes_by_lane(modes, slots, count, lanes):
    width = count // len(slots)
    lane = lax.rem(lax.broadcasted_iota(jnp.int32, (8, lanes), 1), count)
    mode = jnp.zeros((8, lanes), jnp.int32)
    for i in range(count):
        mode = jnp.where(lane == i, modes[slots[i // width] * width + i % width], mode)
    return mode[:1]


def modes_by_row(modes, slots, count, lanes):
    width = count // len(slots)
    row = lax.broadcasted_iota(jnp.int32, (count, lanes), 0)
    mode = jnp.zeros((count, lanes), jnp.int32)
    for i in range(count):
        mode = jnp.where(row == i, modes[slots[i // width] * width + i % width], mode)
    return mode


def phi_slots(n_phi):
    return [slot ^ lax.axis_index("phi") for slot in range(n_phi)]


def gz_slots(n_gz):
    return [slot ^ lax.axis_index("gz") for slot in gz_order(n_gz)]


def build_tables(z_modes, phi_modes, phi_ref, z_ref, n_gz, n_phi):
    phi_local, lanes = phi_ref.shape[0] // 2, phi_ref.shape[1] // 2
    z_local = z_ref.shape[1] // 3
    kp, kz = lanes // 2, z_ref.shape[0] // 2
    n = n_phi * phi_local
    mode = modes_by_lane(phi_modes, phi_slots(n_phi), kp, lanes)
    lane = lax.broadcasted_iota(jnp.int32, (1, lanes), 1)
    quarter = jnp.where(lane < kp, 0, n // 4)
    position = lax.axis_index("phi") * phi_local + lax.broadcasted_iota(jnp.int32, (phi_local, lanes), 0)
    high, low = halves(cosines(position * mode + quarter, n))
    phi_ref[:phi_local, :lanes] = high
    phi_ref[:phi_local, lanes:] = low
    phi_ref[phi_local:, :lanes] = high
    phi_ref[phi_local:, lanes:] = jnp.zeros_like(low)

    n = n_gz * z_local
    mode = modes_by_row(z_modes, gz_slots(n_gz), kz, z_local)
    position = lax.axis_index("gz") * z_local + lax.broadcasted_iota(jnp.int32, (kz, z_local), 1)
    for part, quarter in enumerate((0, 3 * n // 4)):
        high, low = halves(cosines(position * mode + quarter, n))
        for i, term in enumerate((high, low, high)):
            z_ref[part * kz : (part + 1) * kz, i * z_local : (i + 1) * z_local] = term


def forward_kernel(
    z_modes, phi_modes, x_ref, t_ref, ak_ref, as_ref, bk_ref, bs_ref, phi_ref, z_ref, *, n_gz, n_phi
):
    at, count = pl.program_id(0), pl.num_programs(0)

    @pl.when(at == 0)
    def _():
        build_tables(z_modes, phi_modes, phi_ref, z_ref, n_gz, n_phi)

    width = phi_ref.shape[1] // (4 * n_phi)
    for first, keep_ref, send_ref in ((True, ak_ref, as_ref), (False, bk_ref, bs_ref)):

        @pl.when((at < count // 2) == first)
        def _():
            base = (at if first else at - count // 2) * x_ref.shape[0]
            transform(phi_ref, z_ref, x_ref, t_ref, keep_ref, send_ref, base, n_phi, width)


def transform(phi_ref, z_ref, x_ref, t_ref, keep_ref, send_ref, base, n_phi, width):
    block, cycles, z_local, phi_local = x_ref.shape
    modes = z_ref.shape[0] // 2
    lanes = phi_ref.shape[1] // 2
    shape = keep_ref.shape[1:-4] + keep_ref.shape[-2:]
    lane = lax.broadcasted_iota(jnp.int32, (modes, lanes), 1)
    sign = jnp.where(lane < lanes // 2, 1.0, -1.0).astype(f32)

    def along_phi(c, part):
        x = (x_ref, t_ref)[part][c].reshape(cycles * z_local, phi_local)
        high, low = halves(x)
        y = dot(jnp.concatenate([high, low], axis=1), phi_ref[...])
        high, low = (
            jnp.concatenate([term[r * z_local : (r + 1) * z_local] for r in range(cycles)], axis=1)
            for term in halves(y[:, :lanes] + y[:, lanes:])
        )
        return jnp.concatenate([high, high, low], axis=0)

    def along_z(y):
        m = dot(z_ref[...], y)
        return [m[:, r * lanes : (r + 1) * lanes] for r in range(cycles)]

    def finish(c, products):
        items = []
        for m in products:
            items.append(m[:modes] + sign * pltpu.roll(m[modes:], lanes // 2, 1))
        for group in range(len(items) // n_phi):
            part = exchange(items[group * n_phi : (group + 1) * n_phi], width)
            for slot, item in enumerate(part):
                out = keep_ref if slot % 2 == 0 else send_ref
                out[slot // 2, :, base + c, group, :, :] = item.reshape(shape)

    steps = [(c, part) for c in range(block) for part in range(2)]
    ahead = along_phi(*steps[0])
    products = []
    for i, (c, part) in enumerate(steps):
        y = ahead
        if i + 1 < len(steps):
            ahead = along_phi(*steps[i + 1])
        products.append(along_z(y))
        if part == 0 and c:
            finish(c - 1, products[-3] + products[-2])
    finish(block - 1, products[-2] + products[-1])


def forward(field, tangent, z_modes, phi_modes, n_phi, n_gz):
    channels, cycles, z_local, phi_local = field.shape
    groups = 2 * cycles // n_phi
    kz, kp = z_modes.shape[0], phi_modes.shape[0]
    lanes = 2 * kp
    out = pltpu.VMEM((n_phi // 2, n_gz, channels // 2, groups, kz // n_gz, lanes), f32)
    step = 4
    block = pl.BlockSpec((step, cycles, z_local, phi_local), lambda c: (c, 0, 0, 0))
    return pl.pallas_call(
        functools.partial(forward_kernel, n_gz=n_gz, n_phi=n_phi),
        grid=(channels // step,),
        in_specs=[pl.BlockSpec(memory_space=pltpu.SMEM)] * 2 + [block, block],
        out_specs=[pl.BlockSpec(memory_space=pltpu.VMEM)] * 4,
        out_shape=[out] * 4,
        scratch_shapes=[
            pltpu.VMEM((2 * phi_local, 2 * lanes), bf16),
            pltpu.VMEM((2 * kz, 3 * z_local), bf16),
        ],
        compiler_params=pltpu.CompilerParams(vmem_limit_bytes=54 * MIB),
        cost_estimate=pl.CostEstimate(
            flops=24 * field.size * lanes, bytes_accessed=8 * field.size, transcendentals=0
        ),
        name="forward_transform",
    )(z_modes, phi_modes, field, tangent)


def local_kernel(x_ref, t_ref, w_ref, bias_ref, xo_ref, to_ref):
    channels, _, rows, columns = x_ref.shape
    base = pl.multiple_of(pl.program_id(0) * rows, rows)
    tiles = [
        (ref, out, start) for ref, out in ((x_ref, xo_ref), (t_ref, to_ref)) for start in range(0, rows, 8)
    ]
    for at in range(0, len(tiles), 4):
        products = []
        for ref, _, start in tiles[at : at + 4]:
            high, low = halves(ref[:, 0, start : start + 8, :].reshape(channels * 8, columns))
            products.append(dot(w_ref[...], jnp.concatenate([high, low], axis=0)))
        for (_, out, start), m in zip(tiles[at : at + 4], products):
            m = (m[: channels * 8] + m[channels * 8 :]).reshape(channels, 8, columns)
            out[:, pl.ds(base + start, 8), :] = m + bias_ref[...] if out is xo_ref else m


def local_mix(field, tangent, weight, bias, cycle, part, parts):
    channels, _, z_local, phi_local = field.shape
    span = z_local // parts
    rows = min(64, span)
    steps = span // rows
    out = pltpu.VMEM((channels, span, phi_local), f32)
    block = pl.BlockSpec((channels, 1, rows, phi_local), lambda z: (0, cycle, part * steps + z, 0))
    out_block = pl.BlockSpec(memory_space=pltpu.VMEM)
    size = channels * span * phi_local
    return pl.pallas_call(
        local_kernel,
        grid=(steps,),
        in_specs=[
            block,
            block,
            pl.BlockSpec(weight.shape, lambda z: (0, 0)),
            pl.BlockSpec(bias.shape, lambda z: (0, 0, 0)),
        ],
        out_specs=[out_block, out_block],
        out_shape=[out, out],
        compiler_params=pltpu.CompilerParams(vmem_limit_bytes=16 * MIB),
        cost_estimate=pl.CostEstimate(flops=1024 * size, bytes_accessed=8 * size, transcendentals=0),
        name="local_mix",
    )(field, tangent, weight, bias)


def mix_kernel(s_ref, wr_ref, wi_ref, out_ref):
    channels = s_ref.shape[0]
    lanes = s_ref.shape[-1]
    total = jnp.zeros(out_ref.shape, f32)
    for c in range(channels):
        s = s_ref[c]
        turned = jnp.concatenate([s[..., lanes // 2 :], s[..., : lanes // 2]], axis=-1)
        total = total + s[None] * wr_ref[c][:, None] + turned[None] * wi_ref[c][:, None]
    out_ref[...] = total


def mix(spectrum, wr, wi):
    return pl.pallas_call(
        mix_kernel,
        out_shape=jax.ShapeDtypeStruct((wr.shape[1],) + spectrum.shape[1:], f32),
        compiler_params=pltpu.CompilerParams(vmem_limit_bytes=8 * MIB),
        name="mode_mix",
    )(spectrum, wr, wi)


def gelu_pair(x, t):
    a = math.sqrt(2.0 / math.pi)
    b = a * 0.044715
    square = x * x
    s = 0.5 + 0.5 * jnp.tanh(x * (a + b * square))
    out = x * s
    return out, t * (s + out * ((1.0 - s) * (2.0 * a + (6.0 * b) * square)))


def inverse_kernel(*refs, n_phi, width):
    own, other = refs[:6], refs[6:12]
    phi_ref, z_ref = refs[12:14]
    out_ref, out_t_ref = refs[-2:]
    refs = refs[14:-2]
    block, cycles, z_local, phi_local = out_ref.shape
    parts = len(refs) // (2 * cycles)
    span = z_local // parts
    groups, depth, lanes = own[0].shape[-3:]
    modes = z_ref.shape[1] // 6
    first = pl.program_id(0) < pl.num_programs(0) // 2
    at = pl.program_id(0) * block

    def slots(pieces, c, group):
        v, ab1, a20, a21, b20, b21 = pieces
        half = a20.shape[1]
        a_at, b_at = jnp.minimum(at + c, half - 1), jnp.maximum(at + c - half, 0)
        ab1 = ab1[:, at + c, group]
        low = [v[:, at + c, group], jnp.where(first, ab1, b20[:, b_at, group])]
        high = [
            jnp.where(first, a20[:, a_at, group], ab1),
            jnp.where(first, a21[:, a_at, group], b21[:, b_at, group]),
        ]
        return [jnp.concatenate(rows, axis=0).reshape(modes, lanes) for rows in (low, high)]

    for c in range(block):
        spectral = []
        for group in range(groups):
            pairs = zip(slots(own, c, group), slots(other, c, group))
            items = [item for pair in pairs for item in pair]
            high, low = halves(jnp.concatenate(exchange(items, width), axis=0))
            h = dot(jnp.concatenate([high, low, high], axis=1), phi_ref[...])
            for b in range(n_phi):
                part = h[b * modes : (b + 1) * modes]
                part = jnp.concatenate([part[:, :phi_local], part[:, phi_local:]], axis=0)
                high, low = halves(part)
                spectral.append(jnp.concatenate([high, high, low], axis=0))
        values = [dot(z_ref[...], part) for part in spectral]
        for r in range(cycles):
            for p in range(parts):
                rows = slice(p * span, (p + 1) * span)
                lx, lt = refs[2 * (r * parts + p) : 2 * (r * parts + p) + 2]
                x = values[r][rows] + lx[at + c]
                t = values[cycles + r][rows] + lt[at + c]
                out_ref[c, r, rows], out_t_ref[c, r, rows] = gelu_pair(x, t)


def inverse(own, other, phi_table, z_table, local, cycles, n_phi, width):
    channels, span, phi_local = local[0].shape
    z_local = span * len(local) // (2 * cycles)
    step = 2
    steps = channels // step
    held = pl.BlockSpec(memory_space=pltpu.VMEM)
    own, other, local = (
        [pltpu.with_memory_space_constraint(piece, pltpu.VMEM) for piece in pieces]
        for pieces in (own, other, local)
    )
    out = jax.ShapeDtypeStruct((channels, cycles, z_local, phi_local), f32)
    out_block = pl.BlockSpec((step, cycles, z_local, phi_local), lambda o: (o, 0, 0, 0))
    size = channels * cycles * z_local * phi_local
    return pl.pallas_call(
        functools.partial(inverse_kernel, n_phi=n_phi, width=width),
        grid=(steps,),
        in_specs=[held] * 12
        + [
            pl.BlockSpec(phi_table.shape, lambda o: (0, 0)),
            pl.BlockSpec(z_table.shape, lambda o: (0, 0)),
        ]
        + [held] * len(local),
        out_specs=[out_block, out_block],
        out_shape=[out, out],
        compiler_params=pltpu.CompilerParams(vmem_limit_bytes=18 * MIB),
        cost_estimate=pl.CostEstimate(
            flops=1600 * size, bytes_accessed=16 * size, transcendentals=size
        ),
        name="inverse_transform",
    )(*own, *other, phi_table, z_table, *local)


def swap(x, axis, bit):
    count = lax.axis_size(axis)
    return lax.ppermute(x, axis, [(i, i ^ bit) for i in range(count)])


class Filler:
    def __init__(self, field, tangent, small, prepare, parts):
        self.inputs = (field, tangent)
        self.small = small
        self.prepare = prepare
        self.tables = None
        self.parts = parts
        self.todo = [(r, p) for r in range(field.shape[1]) for p in range(parts)]
        self.done = []

    def beside(self, sent, got, count=1):
        if self.tables is None:
            small, _ = lax.optimization_barrier((self.small, sent))
            self.tables = self.prepare(*small)
        for _ in range(min(count, len(self.todo))):
            r, p = self.todo.pop(0)
            inputs, _ = lax.optimization_barrier((self.inputs, sent))
            piece = local_mix(*inputs, *self.tables[:2], r, p, self.parts)
            got, piece = lax.optimization_barrier((got, piece))
            self.done += piece
        return got


def sums_kernel(*refs, outputs):
    refs, outs = refs[: -len(outputs)], refs[-len(outputs) :]
    for out, parts in zip(outs, outputs):
        total = [functools.reduce(jnp.add, [refs[at][index] for at, index in part]) for part in parts]
        out[...] = total[0] if len(total) == 1 else jnp.concatenate(total, axis=1)


def sums(*outputs):
    arrays = []
    plan = []
    shapes = []
    for parts in outputs:
        entry = []
        for part in parts:
            terms = []
            for array, index in part:
                known = [i for i, other in enumerate(arrays) if other is array]
                if not known:
                    known = [len(arrays)]
                    arrays.append(array)
                terms.append((known[0], index))
            entry.append(terms)
        plan.append(entry)
        shape = list(jax.eval_shape(lambda x: x[parts[0][0][1]], parts[0][0][0]).shape)
        if len(parts) > 1:
            shape[1] *= len(parts)
        shapes.append(pltpu.VMEM(tuple(shape), f32))
    return pl.pallas_call(
        functools.partial(sums_kernel, outputs=plan),
        in_specs=[pl.BlockSpec(memory_space=pltpu.VMEM)] * len(arrays),
        out_specs=[pl.BlockSpec(memory_space=pltpu.VMEM)] * len(shapes),
        out_shape=shapes,
        compiler_params=pltpu.CompilerParams(vmem_limit_bytes=8 * MIB),
        name="add_terms",
    )(*[pltpu.with_memory_space_constraint(array, pltpu.VMEM) for array in arrays])


def reduce_scatter(a, b, n_phi, n_gz, filler):
    every, low, high = slice(None), slice(n_gz // 2), slice(n_gz // 2, None)
    a = [a[0], swap(a[1], "phi", 1)]
    b = [b[0], swap(b[1], "phi", 1)]
    (a_sent,) = sums([[(term, (1,)) for term in a]])
    (b_sent,) = sums([[(term, (every, high)) for term in b]])
    got = (swap(a_sent, "phi", 2), swap(b_sent, "gz", 1))
    a_got, b_got = filler.beside((a_sent, b_sent), got, 2)
    a_sent, b_sent = sums(
        [[(term, (0, high)) for term in a] + [(a_got, (high,))]],
        [[(term, (1, low)) for term in b] + [(b_got, (1,))]],
    )
    got = (swap(a_sent, "gz", 1), swap(b_sent, "phi", 2))
    a_new, b_new = filler.beside((a_sent, b_sent), got)

    def rest(i, size):
        rows = slice(i * size, (i + 1) * size)
        return [
            [(term, (0, rows)) for term in a] + [(a_got, (rows,)), (a_new, (rows,))],
            [(term, (0, rows)) for term in b] + [(b_got, (0, rows)), (b_new, (rows,))],
        ]

    left = n_gz // 2
    for bits in gz_groups(n_gz):
        count = 1 << len(bits)
        size = left // count
        v, *sent = sums(*[rest(i, size) for i in range(count)])
        got = [swap(part, "gz", group_bits(i, bits)) for i, part in enumerate(sent, 1)]
        terms = [v, *filler.beside(sent, got, count // 2)]
        rest = lambda i, size: [[(term, (slice(i * size, (i + 1) * size),)) for term in terms]]
        left = size
    return functools.reduce(jnp.add, terms)[0]


def all_gather(v, n_phi, n_gz, filler):
    v = v[None]
    for bits in reversed(gz_groups(n_gz)):
        count = 1 << len(bits)
        got = [swap(v, "gz", group_bits(i, bits)) for i in range(1, count)]
        got = filler.beside(v, got, count // 2)
        v = jnp.concatenate([v, *got], axis=0)
    half = v.shape[1] // 2
    a, b = v[:, :half], v[:, half:]
    first = (swap(a, "gz", 1), swap(b, "phi", 2))
    a20, b20, v_core = swap(a, "phi", 2), swap(b, "gz", 1), swap(v, "phi", 1)
    a1, b1 = filler.beside((a, b), first, len(filler.todo))
    ab1 = jnp.concatenate([a1, b1], axis=1)
    a21, b21 = swap(a1, "phi", 2), swap(b1, "gz", 1)
    ab1_core, a20_core, b20_core = (swap(part, "phi", 1) for part in (ab1, a20, b20))
    a21_core, b21_core = swap(a21, "phi", 1), swap(b21, "phi", 1)
    return (v, ab1, a20, a21, b20, b21), (v_core, ab1_core, a20_core, a21_core, b20_core, b21_core)


def gz_groups(n_gz):
    bits = list(range(1, n_gz.bit_length() - 1))
    return [bits[i : i + 2] for i in range(0, len(bits), 2)]


def group_bits(i, bits):
    digits = [(i >> (len(bits) - 1 - j)) & 1 for j in range(len(bits))]
    return sum(digit << bit for digit, bit in zip(digits, bits))


def gz_order(n_gz):
    bits = n_gz.bit_length() - 1
    return [
        sum(digit << i for i, digit in enumerate(digits))
        for digits in itertools.product((0, 1), repeat=bits)
    ]


def tables_kernel(
    z_modes, phi_modes, bias, weight_ref, modes_ref, local_ref, bias_ref, phi_ref, z_ref, wr_ref, wi_ref,
    *, n_gz, n_phi, scale
):
    channels = weight_ref.shape[0]
    rows = 8 * channels
    row = lax.broadcasted_iota(jnp.int32, (rows, channels), 0)
    copy = (row // 8 == lax.broadcasted_iota(jnp.int32, (rows, channels), 1)).astype(bf16)
    row = lax.broadcasted_iota(jnp.int32, (rows, rows), 0)
    column = lax.broadcasted_iota(jnp.int32, (rows, rows), 1)
    same = lax.rem(row, 8) == lax.rem(column, 8)
    last = (((1,), (1,)), ((), ()))
    for part, w in enumerate(halves(weight_ref[...])):
        wide = lax.dot_general(copy, w, last, preferred_element_type=f32).astype(bf16)
        wide = lax.dot_general(wide, copy, last, preferred_element_type=f32)
        wide = jnp.where(same, wide, 0.0).astype(bf16)
        local_ref[part * rows : (part + 1) * rows, :rows] = wide
        local_ref[part * rows : (part + 1) * rows, rows:] = wide
    for o in range(channels):
        bias_ref[o] = jnp.full(bias_ref.shape[1:], bias[o], f32)

    lanes = phi_ref.shape[0] // 3
    phi_local = phi_ref.shape[1] // 2
    kp = lanes // 2
    n = n_phi * phi_local
    mode = modes_by_row(phi_modes, phi_slots(n_phi), kp, phi_local)
    position = lax.axis_index("phi") * phi_local + lax.broadcasted_iota(jnp.int32, (kp, phi_local), 1)
    turns = position * mode
    cosine = halves(cosines(turns, n))
    sine = halves(cosines(turns + 3 * n // 4, n))
    minus = halves(cosines(turns + n // 4, n))
    for i, part in enumerate((0, 0, 1)):
        at = i * lanes
        phi_ref[at : at + kp, :phi_local] = cosine[part]
        phi_ref[at : at + kp, phi_local:] = sine[part]
        phi_ref[at + kp : at + lanes, :phi_local] = minus[part]
        phi_ref[at + kp : at + lanes, phi_local:] = cosine[part]

    z_local, both = z_ref.shape[0], z_ref.shape[1] // 3
    kz = both // 2
    n = n_gz * z_local
    mode = modes_by_lane(z_modes, gz_slots(n_gz), kz, both)
    quarter = jnp.where(lax.broadcasted_iota(jnp.int32, (1, both), 1) < kz, 0, n // 4)
    position = lax.axis_index("gz") * z_local + lax.broadcasted_iota(jnp.int32, (z_local, both), 0)
    high, low = halves(cosines(position * mode + quarter, n))
    for i, part in enumerate((high, low, high)):
        z_ref[:, i * both : (i + 1) * both] = part

    width = kp // n_phi
    lane = lax.broadcasted_iota(jnp.int32, (width, lanes), 1)
    copy = (lax.rem(lane, width) == lax.broadcasted_iota(jnp.int32, (width, lanes), 0)).astype(bf16)
    sign = jnp.where(lax.broadcasted_iota(jnp.int32, (1, lanes), 1) < kp, -scale, scale).astype(f32)
    for part, (out, factor) in enumerate(((wr_ref, scale), (wi_ref, sign))):
        left = modes_ref[part]
        total = jnp.zeros(out.shape, f32)
        for _ in range(3):
            term = left.astype(bf16)
            left = left - term.astype(f32)
            total = total + dot(term, copy)
        out[...] = total * factor


def tables(spectral_weight, local_weight, bias_term, z_modes, phi_modes, z_local, phi_local):
    n_gz = lax.axis_size("gz")
    n_phi = lax.axis_size("phi")
    kz, kp = z_modes.shape[0], phi_modes.shape[0]
    channels = local_weight.shape[0]
    depth, width = spectral_weight.shape[-2:]
    rows = channels * channels * depth
    scale = (1.0 / math.sqrt(z_local * n_gz * phi_local * n_phi)) * (2.0 / math.sqrt(kz * kp))
    vmem, smem = pl.BlockSpec(memory_space=pltpu.VMEM), pl.BlockSpec(memory_space=pltpu.SMEM)
    *result, wr, wi = pl.pallas_call(
        functools.partial(tables_kernel, n_gz=n_gz, n_phi=n_phi, scale=scale),
        in_specs=[smem, smem, smem, vmem, vmem],
        out_specs=[vmem] * 6,
        out_shape=[
            jax.ShapeDtypeStruct((16 * channels, 16 * channels), bf16),
            jax.ShapeDtypeStruct((channels, 8, phi_local), f32),
            jax.ShapeDtypeStruct((6 * kp, 2 * phi_local), bf16),
            jax.ShapeDtypeStruct((z_local, 6 * kz), bf16),
            jax.ShapeDtypeStruct((rows, 2 * kp), f32),
            jax.ShapeDtypeStruct((rows, 2 * kp), f32),
        ],
        compiler_params=pltpu.CompilerParams(vmem_limit_bytes=16 * MIB),
        name="small_tables",
    )(z_modes, phi_modes, bias_term, local_weight, spectral_weight.reshape(2, rows, width))
    shape = (channels, channels, depth, 2 * kp)
    return *result, wr.reshape(shape), wi.reshape(shape)


def body(field, field_tangent, spectral_weight, local_weight, bias_term, z_modes, phi_modes):
    channels, cycles, z_local, phi_local = field.shape
    n_gz = lax.axis_size("gz")
    n_phi = lax.axis_size("phi")
    width = phi_modes.shape[0] // n_phi
    small = (spectral_weight, local_weight, bias_term, z_modes, phi_modes)
    prepare = functools.partial(tables, z_local=z_local, phi_local=phi_local)
    field = pltpu.with_memory_space_constraint(field, pltpu.HBM)
    field_tangent = pltpu.with_memory_space_constraint(field_tangent, pltpu.HBM)
    filler = Filler(field, field_tangent, small, prepare, 2)

    ak, asent, bk, bsent = forward(field, field_tangent, z_modes, phi_modes, n_phi, n_gz)
    spectrum = reduce_scatter((ak, asent), (bk, bsent), n_phi, n_gz, filler)
    _, _, phi_back, z_back, wr, wi = filler.tables
    mixed = mix(spectrum, wr, wi)
    own, other = all_gather(mixed, n_phi, n_gz, filler)
    return inverse(own, other, phi_back, z_back, filler.done, cycles, n_phi, width)


def solution(mesh):
    return jax.shard_map(
        body,
        mesh=mesh,
        in_specs=(
            P(None, None, "gz", "phi"),
            P(None, None, "gz", "phi"),
            P(None, None, None, "gz", "phi"),
            P(),
            P(),
            P(),
            P(),
        ),
        out_specs=(P(None, None, "gz", "phi"), P(None, None, "gz", "phi")),
        check_vma=False,
    )
```

```python
import functools
import itertools
import math

import jax
import jax.numpy as jnp
from jax import lax
from jax.experimental import pallas as pl
from jax.experimental.pallas import tpu as pltpu
from jax.sharding import PartitionSpec as P

f32 = jnp.float32
bf16 = jnp.bfloat16
MIB = 1024 * 1024


def halves(x):
    high = x.astype(bf16)
    return high, (x - high.astype(f32)).astype(bf16)


def dot(a, b):
    return lax.dot_general(a, b, (((1,), (0,)), ((), ())), preferred_element_type=f32)


def exchange(items, width):
    items = list(items)
    count = len(items)
    lanes = items[0].shape[-1]
    lane = lax.broadcasted_iota(jnp.int32, items[0].shape, items[0].ndim - 1)
    step = 1
    while step < count:
        shift = width * step
        low = (lane // shift) % 2 == 0
        for i in range(count):
            if i & step:
                continue
            a, b = items[i], items[i | step]
            items[i] = jnp.where(low, a, pltpu.roll(b, shift, 1))
            items[i | step] = jnp.where(low, pltpu.roll(a, lanes - shift, 1), b)
        step *= 2
    return items


def wrap(x, n):
    return x & (n - 1) if n & (n - 1) == 0 else lax.rem(x, n)


def cosines(turns, n):
    return jnp.cos(wrap(turns, n).astype(f32) * (2.0 * math.pi / n))


def modes_by_lane(modes, slots, count, lanes):
    width = count // len(slots)
    lane = lax.rem(lax.broadcasted_iota(jnp.int32, (8, lanes), 1), count)
    mode = jnp.zeros((8, lanes), jnp.int32)
    for i in range(count):
        mode = jnp.where(lane == i, modes[slots[i // width] * width + i % width], mode)
    return mode[:1]


def modes_by_row(modes, slots, count, lanes):
    width = count // len(slots)
    row = lax.broadcasted_iota(jnp.int32, (count, lanes), 0)
    mode = jnp.zeros((count, lanes), jnp.int32)
    for i in range(count):
        mode = jnp.where(row == i, modes[slots[i // width] * width + i % width], mode)
    return mode


def phi_slots(n_phi):
    return [slot ^ lax.axis_index("phi") for slot in range(n_phi)]


def gz_slots(n_gz):
    return [slot ^ lax.axis_index("gz") for slot in gz_order(n_gz)]


def build_tables(z_modes, phi_modes, phi_ref, z_ref, n_gz, n_phi):
    phi_local, lanes = phi_ref.shape[0] // 2, phi_ref.shape[1] // 2
    z_local = z_ref.shape[1] // 3
    kp, kz = lanes // 2, z_ref.shape[0] // 2
    n = n_phi * phi_local
    mode = modes_by_lane(phi_modes, phi_slots(n_phi), kp, lanes)
    lane = lax.broadcasted_iota(jnp.int32, (1, lanes), 1)
    quarter = jnp.where(lane < kp, 0, n // 4)
    position = lax.axis_index("phi") * phi_local + lax.broadcasted_iota(jnp.int32, (phi_local, lanes), 0)
    high, low = halves(cosines(position * mode + quarter, n))
    phi_ref[:phi_local, :lanes] = high
    phi_ref[:phi_local, lanes:] = low
    phi_ref[phi_local:, :lanes] = high
    phi_ref[phi_local:, lanes:] = jnp.zeros_like(low)

    n = n_gz * z_local
    mode = modes_by_row(z_modes, gz_slots(n_gz), kz, z_local)
    position = lax.axis_index("gz") * z_local + lax.broadcasted_iota(jnp.int32, (kz, z_local), 1)
    for part, quarter in enumerate((0, 3 * n // 4)):
        high, low = halves(cosines(position * mode + quarter, n))
        for i, term in enumerate((high, low, high)):
            z_ref[part * kz : (part + 1) * kz, i * z_local : (i + 1) * z_local] = term


def forward_kernel(
    z_modes, phi_modes, x_ref, t_ref, ak_ref, as_ref, bk_ref, bs_ref, phi_ref, z_ref, *, n_gz, n_phi
):
    at, count = pl.program_id(0), pl.num_programs(0)

    @pl.when(at == 0)
    def _():
        build_tables(z_modes, phi_modes, phi_ref, z_ref, n_gz, n_phi)

    width = phi_ref.shape[1] // (4 * n_phi)
    for first, keep_ref, send_ref in ((True, ak_ref, as_ref), (False, bk_ref, bs_ref)):

        @pl.when((at < count // 2) == first)
        def _():
            base = (at if first else at - count // 2) * x_ref.shape[0]
            transform(phi_ref, z_ref, x_ref, t_ref, keep_ref, send_ref, base, n_phi, width)


def transform(phi_ref, z_ref, x_ref, t_ref, keep_ref, send_ref, base, n_phi, width):
    block, cycles, z_local, phi_local = x_ref.shape
    modes = z_ref.shape[0] // 2
    lanes = phi_ref.shape[1] // 2
    shape = keep_ref.shape[1:-4] + keep_ref.shape[-2:]
    lane = lax.broadcasted_iota(jnp.int32, (modes, lanes), 1)
    sign = jnp.where(lane < lanes // 2, 1.0, -1.0).astype(f32)

    def along_phi(c, part):
        x = (x_ref, t_ref)[part][c].reshape(cycles * z_local, phi_local)
        high, low = halves(x)
        y = dot(jnp.concatenate([high, low], axis=1), phi_ref[...])
        high, low = (
            jnp.concatenate([term[r * z_local : (r + 1) * z_local] for r in range(cycles)], axis=1)
            for term in halves(y[:, :lanes] + y[:, lanes:])
        )
        return jnp.concatenate([high, high, low], axis=0)

    def along_z(y):
        m = dot(z_ref[...], y)
        return [m[:, r * lanes : (r + 1) * lanes] for r in range(cycles)]

    def finish(c, products):
        items = []
        for m in products:
            items.append(m[:modes] + sign * pltpu.roll(m[modes:], lanes // 2, 1))
        for group in range(len(items) // n_phi):
            part = exchange(items[group * n_phi : (group + 1) * n_phi], width)
            for slot, item in enumerate(part):
                out = keep_ref if slot % 2 == 0 else send_ref
                out[slot // 2, :, base + c, group, :, :] = item.reshape(shape)

    steps = [(c, part) for c in range(block) for part in range(2)]
    ahead = along_phi(*steps[0])
    products = []
    for i, (c, part) in enumerate(steps):
        y = ahead
        if i + 1 < len(steps):
            ahead = along_phi(*steps[i + 1])
        products.append(along_z(y))
        if part == 0 and c:
            finish(c - 1, products[-3] + products[-2])
    finish(block - 1, products[-2] + products[-1])


def forward(field, tangent, z_modes, phi_modes, n_phi, n_gz):
    channels, cycles, z_local, phi_local = field.shape
    groups = 2 * cycles // n_phi
    kz, kp = z_modes.shape[0], phi_modes.shape[0]
    lanes = 2 * kp
    out = pltpu.VMEM((n_phi // 2, n_gz, channels // 2, groups, kz // n_gz, lanes), f32)
    step = 4
    block = pl.BlockSpec((step, cycles, z_local, phi_local), lambda c: (c, 0, 0, 0))
    return pl.pallas_call(
        functools.partial(forward_kernel, n_gz=n_gz, n_phi=n_phi),
        grid=(channels // step,),
        in_specs=[pl.BlockSpec(memory_space=pltpu.SMEM)] * 2 + [block, block],
        out_specs=[pl.BlockSpec(memory_space=pltpu.VMEM)] * 4,
        out_shape=[out] * 4,
        scratch_shapes=[
            pltpu.VMEM((2 * phi_local, 2 * lanes), bf16),
            pltpu.VMEM((2 * kz, 3 * z_local), bf16),
        ],
        compiler_params=pltpu.CompilerParams(vmem_limit_bytes=54 * MIB),
        cost_estimate=pl.CostEstimate(
            flops=24 * field.size * lanes, bytes_accessed=8 * field.size, transcendentals=0
        ),
        name="forward_transform",
    )(z_modes, phi_modes, field, tangent)


def local_kernel(x_ref, t_ref, w_ref, bias_ref, xo_ref, to_ref):
    channels, _, rows, columns = x_ref.shape
    base = pl.multiple_of(pl.program_id(0) * rows, rows)
    tiles = [
        (ref, out, start) for ref, out in ((x_ref, xo_ref), (t_ref, to_ref)) for start in range(0, rows, 8)
    ]
    for at in range(0, len(tiles), 4):
        products = []
        for ref, _, start in tiles[at : at + 4]:
            high, low = halves(ref[:, 0, start : start + 8, :].reshape(channels * 8, columns))
            products.append(dot(w_ref[...], jnp.concatenate([high, low], axis=0)))
        for (_, out, start), m in zip(tiles[at : at + 4], products):
            m = (m[: channels * 8] + m[channels * 8 :]).reshape(channels, 8, columns)
            out[:, pl.ds(base + start, 8), :] = m + bias_ref[...] if out is xo_ref else m


def local_mix(field, tangent, weight, bias, cycle, part, parts):
    channels, _, z_local, phi_local = field.shape
    span = z_local // parts
    rows = min(64, span)
    steps = span // rows
    out = pltpu.VMEM((channels, span, phi_local), f32)
    block = pl.BlockSpec((channels, 1, rows, phi_local), lambda z: (0, cycle, part * steps + z, 0))
    out_block = pl.BlockSpec(memory_space=pltpu.VMEM)
    size = channels * span * phi_local
    return pl.pallas_call(
        local_kernel,
        grid=(steps,),
        in_specs=[
            block,
            block,
            pl.BlockSpec(weight.shape, lambda z: (0, 0)),
            pl.BlockSpec(bias.shape, lambda z: (0, 0, 0)),
        ],
        out_specs=[out_block, out_block],
        out_shape=[out, out],
        compiler_params=pltpu.CompilerParams(vmem_limit_bytes=16 * MIB),
        cost_estimate=pl.CostEstimate(flops=1024 * size, bytes_accessed=8 * size, transcendentals=0),
        name="local_mix",
    )(field, tangent, weight, bias)


def mix_kernel(s_ref, wr_ref, wi_ref, out_ref):
    channels = s_ref.shape[0]
    lanes = s_ref.shape[-1]
    total = jnp.zeros(out_ref.shape, f32)
    for c in range(channels):
        s = s_ref[c]
        turned = jnp.concatenate([s[..., lanes // 2 :], s[..., : lanes // 2]], axis=-1)
        total = total + s[None] * wr_ref[c][:, None] + turned[None] * wi_ref[c][:, None]
    out_ref[...] = total


def mix(spectrum, wr, wi):
    return pl.pallas_call(
        mix_kernel,
        out_shape=jax.ShapeDtypeStruct((wr.shape[1],) + spectrum.shape[1:], f32),
        compiler_params=pltpu.CompilerParams(vmem_limit_bytes=8 * MIB),
        name="mode_mix",
    )(spectrum, wr, wi)


def gelu_pair(x, t):
    a = math.sqrt(2.0 / math.pi)
    b = a * 0.044715
    square = x * x
    s = 0.5 + 0.5 * jnp.tanh(x * (a + b * square))
    out = x * s
    return out, t * (s + out * ((1.0 - s) * (2.0 * a + (6.0 * b) * square)))


def inverse_kernel(*refs, n_phi, width):
    own, other = refs[:6], refs[6:12]
    phi_ref, z_ref = refs[12:14]
    out_ref, out_t_ref = refs[-2:]
    refs = refs[14:-2]
    block, cycles, z_local, phi_local = out_ref.shape
    parts = len(refs) // (2 * cycles)
    span = z_local // parts
    groups, depth, lanes = own[0].shape[-3:]
    modes = z_ref.shape[1] // 6
    first = pl.program_id(0) < pl.num_programs(0) // 2
    at = pl.program_id(0) * block

    def slots(pieces, c, group):
        v, ab1, a20, a21, b20, b21 = pieces
        half = a20.shape[1]
        a_at, b_at = jnp.minimum(at + c, half - 1), jnp.maximum(at + c - half, 0)
        ab1 = ab1[:, at + c, group]
        low = [v[:, at + c, group], jnp.where(first, ab1, b20[:, b_at, group])]
        high = [
            jnp.where(first, a20[:, a_at, group], ab1),
            jnp.where(first, a21[:, a_at, group], b21[:, b_at, group]),
        ]
        return [jnp.concatenate(rows, axis=0).reshape(modes, lanes) for rows in (low, high)]

    for c in range(block):
        spectral = []
        for group in range(groups):
            pairs = zip(slots(own, c, group), slots(other, c, group))
            items = [item for pair in pairs for item in pair]
            high, low = halves(jnp.concatenate(exchange(items, width), axis=0))
            h = dot(jnp.concatenate([high, low, high], axis=1), phi_ref[...])
            for b in range(n_phi):
                part = h[b * modes : (b + 1) * modes]
                part = jnp.concatenate([part[:, :phi_local], part[:, phi_local:]], axis=0)
                high, low = halves(part)
                spectral.append(jnp.concatenate([high, high, low], axis=0))
        values = [dot(z_ref[...], part) for part in spectral]
        for r in range(cycles):
            for p in range(parts):
                rows = slice(p * span, (p + 1) * span)
                lx, lt = refs[2 * (r * parts + p) : 2 * (r * parts + p) + 2]
                x = values[r][rows] + lx[at + c]
                t = values[cycles + r][rows] + lt[at + c]
                out_ref[c, r, rows], out_t_ref[c, r, rows] = gelu_pair(x, t)


def inverse(own, other, phi_table, z_table, local, cycles, n_phi, width):
    channels, span, phi_local = local[0].shape
    z_local = span * len(local) // (2 * cycles)
    step = 2
    steps = channels // step
    held = pl.BlockSpec(memory_space=pltpu.VMEM)
    own, other, local = (
        [pltpu.with_memory_space_constraint(piece, pltpu.VMEM) for piece in pieces]
        for pieces in (own, other, local)
    )
    out = jax.ShapeDtypeStruct((channels, cycles, z_local, phi_local), f32)
    out_block = pl.BlockSpec((step, cycles, z_local, phi_local), lambda o: (o, 0, 0, 0))
    size = channels * cycles * z_local * phi_local
    return pl.pallas_call(
        functools.partial(inverse_kernel, n_phi=n_phi, width=width),
        grid=(steps,),
        in_specs=[held] * 12
        + [
            pl.BlockSpec(phi_table.shape, lambda o: (0, 0)),
            pl.BlockSpec(z_table.shape, lambda o: (0, 0)),
        ]
        + [held] * len(local),
        out_specs=[out_block, out_block],
        out_shape=[out, out],
        compiler_params=pltpu.CompilerParams(vmem_limit_bytes=18 * MIB),
        cost_estimate=pl.CostEstimate(
            flops=1600 * size, bytes_accessed=16 * size, transcendentals=size
        ),
        name="inverse_transform",
    )(*own, *other, phi_table, z_table, *local)


def swap(x, axis, bit):
    count = lax.axis_size(axis)
    return lax.ppermute(x, axis, [(i, i ^ bit) for i in range(count)])


class Filler:
    def __init__(self, field, tangent, small, prepare, parts):
        self.inputs = (field, tangent)
        self.small = small
        self.prepare = prepare
        self.tables = None
        self.parts = parts
        self.todo = [(r, p) for r in range(field.shape[1]) for p in range(parts)]
        self.done = []

    def beside(self, sent, got, count=1):
        if self.tables is None:
            small, _ = lax.optimization_barrier((self.small, sent))
            self.tables = self.prepare(*small)
        for _ in range(min(count, len(self.todo))):
            r, p = self.todo.pop(0)
            inputs, _ = lax.optimization_barrier((self.inputs, sent))
            piece = local_mix(*inputs, *self.tables[:2], r, p, self.parts)
            got, piece = lax.optimization_barrier((got, piece))
            self.done += piece
        return got


def sums_kernel(*refs, outputs):
    refs, outs = refs[: -len(outputs)], refs[-len(outputs) :]
    for out, parts in zip(outs, outputs):
        total = [functools.reduce(jnp.add, [refs[at][index] for at, index in part]) for part in parts]
        out[...] = total[0] if len(total) == 1 else jnp.concatenate(total, axis=1)


def sums(*outputs):
    arrays = []
    plan = []
    shapes = []
    for parts in outputs:
        entry = []
        for part in parts:
            terms = []
            for array, index in part:
                known = [i for i, other in enumerate(arrays) if other is array]
                if not known:
                    known = [len(arrays)]
                    arrays.append(array)
                terms.append((known[0], index))
            entry.append(terms)
        plan.append(entry)
        shape = list(jax.eval_shape(lambda x: x[parts[0][0][1]], parts[0][0][0]).shape)
        if len(parts) > 1:
            shape[1] *= len(parts)
        shapes.append(pltpu.VMEM(tuple(shape), f32))
    return pl.pallas_call(
        functools.partial(sums_kernel, outputs=plan),
        in_specs=[pl.BlockSpec(memory_space=pltpu.VMEM)] * len(arrays),
        out_specs=[pl.BlockSpec(memory_space=pltpu.VMEM)] * len(shapes),
        out_shape=shapes,
        compiler_params=pltpu.CompilerParams(vmem_limit_bytes=8 * MIB),
        name="add_terms",
    )(*[pltpu.with_memory_space_constraint(array, pltpu.VMEM) for array in arrays])


def reduce_scatter(a, b, n_phi, n_gz, filler):
    every, low, high = slice(None), slice(n_gz // 2), slice(n_gz // 2, None)
    a = [a[0], swap(a[1], "phi", 1)]
    b = [b[0], swap(b[1], "phi", 1)]
    a_first, a_last = sums([[(term, (1, high)) for term in a]], [[(term, (1, low)) for term in a]])
    b_first, b_last = sums([[(term, (1, high)) for term in b]], [[(term, (0, high)) for term in b]])
    got = (swap(a_first, "phi", 2), swap(b_first, "gz", 1))
    a_rest, b_rest = swap(a_last, "phi", 2), swap(b_last, "gz", 1)
    a_got, b_got = filler.beside((a_first, b_first), got, 2)
    a_sent, b_sent = sums(
        [[(term, (0, high)) for term in a] + [(a_got, (every,))]],
        [[(term, (1, low)) for term in b] + [(b_got, (every,))]],
    )
    got = (swap(a_sent, "gz", 1), swap(b_sent, "phi", 2))
    a_new, b_new = filler.beside((a_sent, b_sent), got)

    def rest(i, size):
        rows = slice(i * size, (i + 1) * size)
        return [
            [(term, (0, rows)) for term in a] + [(a_rest, (rows,)), (a_new, (rows,))],
            [(term, (0, rows)) for term in b] + [(b_rest, (rows,)), (b_new, (rows,))],
        ]

    left = n_gz // 2
    for bits in gz_groups(n_gz):
        count = 1 << len(bits)
        size = left // count
        v, *sent = sums(*[rest(i, size) for i in range(count)])
        got = [swap(part, "gz", group_bits(i, bits)) for i, part in enumerate(sent, 1)]
        terms = [v, *filler.beside(sent, got, count // 2)]
        rest = lambda i, size: [[(term, (slice(i * size, (i + 1) * size),)) for term in terms]]
        left = size
    return functools.reduce(jnp.add, terms)[0]


def all_gather(v, n_phi, n_gz, filler):
    v = v[None]
    for bits in reversed(gz_groups(n_gz)):
        count = 1 << len(bits)
        got = [swap(v, "gz", group_bits(i, bits)) for i in range(1, count)]
        got = filler.beside(v, got, count // 2)
        v = jnp.concatenate([v, *got], axis=0)
    half = v.shape[1] // 2
    a, b = v[:, :half], v[:, half:]
    first = (swap(a, "gz", 1), swap(b, "phi", 2))
    a20, b20, v_core = swap(a, "phi", 2), swap(b, "gz", 1), swap(v, "phi", 1)
    a1, b1 = filler.beside((a, b), first, len(filler.todo))
    ab1 = jnp.concatenate([a1, b1], axis=1)
    a21, b21 = swap(a1, "phi", 2), swap(b1, "gz", 1)
    ab1_core, a20_core, b20_core = (swap(part, "phi", 1) for part in (ab1, a20, b20))
    a21_core, b21_core = swap(a21, "phi", 1), swap(b21, "phi", 1)
    return (v, ab1, a20, a21, b20, b21), (v_core, ab1_core, a20_core, a21_core, b20_core, b21_core)


def gz_groups(n_gz):
    bits = list(range(1, n_gz.bit_length() - 1))
    return [bits[i : i + 2] for i in range(0, len(bits), 2)]


def group_bits(i, bits):
    digits = [(i >> (len(bits) - 1 - j)) & 1 for j in range(len(bits))]
    return sum(digit << bit for digit, bit in zip(digits, bits))


def gz_order(n_gz):
    bits = n_gz.bit_length() - 1
    return [
        sum(digit << i for i, digit in enumerate(digits))
        for digits in itertools.product((0, 1), repeat=bits)
    ]


def tables_kernel(
    z_modes, phi_modes, bias, weight_ref, modes_ref, local_ref, bias_ref, phi_ref, z_ref, wr_ref, wi_ref,
    *, n_gz, n_phi, scale
):
    channels = weight_ref.shape[0]
    rows = 8 * channels
    row = lax.broadcasted_iota(jnp.int32, (rows, channels), 0)
    copy = (row // 8 == lax.broadcasted_iota(jnp.int32, (rows, channels), 1)).astype(bf16)
    row = lax.broadcasted_iota(jnp.int32, (rows, rows), 0)
    column = lax.broadcasted_iota(jnp.int32, (rows, rows), 1)
    same = lax.rem(row, 8) == lax.rem(column, 8)
    last = (((1,), (1,)), ((), ()))
    for part, w in enumerate(halves(weight_ref[...])):
        wide = lax.dot_general(copy, w, last, preferred_element_type=f32).astype(bf16)
        wide = lax.dot_general(wide, copy, last, preferred_element_type=f32)
        wide = jnp.where(same, wide, 0.0).astype(bf16)
        local_ref[part * rows : (part + 1) * rows, :rows] = wide
        local_ref[part * rows : (part + 1) * rows, rows:] = wide
    for o in range(channels):
        bias_ref[o] = jnp.full(bias_ref.shape[1:], bias[o], f32)

    lanes = phi_ref.shape[0] // 3
    phi_local = phi_ref.shape[1] // 2
    kp = lanes // 2
    n = n_phi * phi_local
    mode = modes_by_row(phi_modes, phi_slots(n_phi), kp, phi_local)
    position = lax.axis_index("phi") * phi_local + lax.broadcasted_iota(jnp.int32, (kp, phi_local), 1)
    turns = position * mode
    cosine = halves(cosines(turns, n))
    sine = halves(cosines(turns + 3 * n // 4, n))
    minus = halves(cosines(turns + n // 4, n))
    for i, part in enumerate((0, 0, 1)):
        at = i * lanes
        phi_ref[at : at + kp, :phi_local] = cosine[part]
        phi_ref[at : at + kp, phi_local:] = sine[part]
        phi_ref[at + kp : at + lanes, :phi_local] = minus[part]
        phi_ref[at + kp : at + lanes, phi_local:] = cosine[part]

    z_local, both = z_ref.shape[0], z_ref.shape[1] // 3
    kz = both // 2
    n = n_gz * z_local
    mode = modes_by_lane(z_modes, gz_slots(n_gz), kz, both)
    quarter = jnp.where(lax.broadcasted_iota(jnp.int32, (1, both), 1) < kz, 0, n // 4)
    position = lax.axis_index("gz") * z_local + lax.broadcasted_iota(jnp.int32, (z_local, both), 0)
    high, low = halves(cosines(position * mode + quarter, n))
    for i, part in enumerate((high, low, high)):
        z_ref[:, i * both : (i + 1) * both] = part

    width = kp // n_phi
    lane = lax.broadcasted_iota(jnp.int32, (width, lanes), 1)
    copy = (lax.rem(lane, width) == lax.broadcasted_iota(jnp.int32, (width, lanes), 0)).astype(bf16)
    sign = jnp.where(lax.broadcasted_iota(jnp.int32, (1, lanes), 1) < kp, -scale, scale).astype(f32)
    for part, (out, factor) in enumerate(((wr_ref, scale), (wi_ref, sign))):
        left = modes_ref[part]
        total = jnp.zeros(out.shape, f32)
        for _ in range(3):
            term = left.astype(bf16)
            left = left - term.astype(f32)
            total = total + dot(term, copy)
        out[...] = total * factor


def tables(spectral_weight, local_weight, bias_term, z_modes, phi_modes, z_local, phi_local):
    n_gz = lax.axis_size("gz")
    n_phi = lax.axis_size("phi")
    kz, kp = z_modes.shape[0], phi_modes.shape[0]
    channels = local_weight.shape[0]
    depth, width = spectral_weight.shape[-2:]
    rows = channels * channels * depth
    scale = (1.0 / math.sqrt(z_local * n_gz * phi_local * n_phi)) * (2.0 / math.sqrt(kz * kp))
    vmem, smem = pl.BlockSpec(memory_space=pltpu.VMEM), pl.BlockSpec(memory_space=pltpu.SMEM)
    *result, wr, wi = pl.pallas_call(
        functools.partial(tables_kernel, n_gz=n_gz, n_phi=n_phi, scale=scale),
        in_specs=[smem, smem, smem, vmem, vmem],
        out_specs=[vmem] * 6,
        out_shape=[
            jax.ShapeDtypeStruct((16 * channels, 16 * channels), bf16),
            jax.ShapeDtypeStruct((channels, 8, phi_local), f32),
            jax.ShapeDtypeStruct((6 * kp, 2 * phi_local), bf16),
            jax.ShapeDtypeStruct((z_local, 6 * kz), bf16),
            jax.ShapeDtypeStruct((rows, 2 * kp), f32),
            jax.ShapeDtypeStruct((rows, 2 * kp), f32),
        ],
        compiler_params=pltpu.CompilerParams(vmem_limit_bytes=16 * MIB),
        name="small_tables",
    )(z_modes, phi_modes, bias_term, local_weight, spectral_weight.reshape(2, rows, width))
    shape = (channels, channels, depth, 2 * kp)
    return *result, wr.reshape(shape), wi.reshape(shape)


def body(field, field_tangent, spectral_weight, local_weight, bias_term, z_modes, phi_modes):
    channels, cycles, z_local, phi_local = field.shape
    n_gz = lax.axis_size("gz")
    n_phi = lax.axis_size("phi")
    width = phi_modes.shape[0] // n_phi
    small = (spectral_weight, local_weight, bias_term, z_modes, phi_modes)
    prepare = functools.partial(tables, z_local=z_local, phi_local=phi_local)
    field = pltpu.with_memory_space_constraint(field, pltpu.HBM)
    field_tangent = pltpu.with_memory_space_constraint(field_tangent, pltpu.HBM)
    filler = Filler(field, field_tangent, small, prepare, 2)

    ak, asent, bk, bsent = forward(field, field_tangent, z_modes, phi_modes, n_phi, n_gz)
    spectrum = reduce_scatter((ak, asent), (bk, bsent), n_phi, n_gz, filler)
    _, _, phi_back, z_back, wr, wi = filler.tables
    mixed = mix(spectrum, wr, wi)
    own, other = all_gather(mixed, n_phi, n_gz, filler)
    return inverse(own, other, phi_back, z_back, filler.done, cycles, n_phi, width)


def solution(mesh):
    return jax.shard_map(
        body,
        mesh=mesh,
        in_specs=(
            P(None, None, "gz", "phi"),
            P(None, None, "gz", "phi"),
            P(None, None, None, "gz", "phi"),
            P(),
            P(),
            P(),
            P(),
        ),
        out_specs=(P(None, None, "gz", "phi"), P(None, None, "gz", "phi")),
        check_vma=False,
    )
```
